32 devices in a mesh: inst: 8 (over z, y), feat: 4 (over x, core).
Axes of the slice: x: 2, y: 2, z: 4, core: 2. Of those that a mesh axis runs over, the one named last changes fastest.
Arguments:
- values: bfloat16 [128, 32, 128, 128], P('inst', 'feat'), may hold values from -0.5 to 0.5
- columns: int32 [128, 32], P('inst', 'feat'), may hold values from 0 to 2047
- live_slots: int32 [128, 4], P('inst', 'feat'), may hold values from 1 to 8, as said below
- labels: int32 [16384], P('inst'), may hold values 0 or 1
- weights: float32 [8192, 128], P('feat'), may hold values from -0.75 to 0.75
Outputs:
- step_vector: float32 [8192, 128], P(('feat', 'inst'))
- gradient: float32 [8192, 128], P(('feat', 'inst'))
The draws below stay inside these ranges and needn't reach their ends.
Inputs may be any that keep to these rules, and one draw needn't show every extreme that they name: Slot j of tile t in feature group g is used when j < live_slots[t, g]; in every draw some tile has 8 used slots in every group. `columns`: block of a slot counted within its feature group's 2048 blocks; slots of one tile may name the same block.
All inputs are finite; a program needn't handle non-finite values. No bound on the sum of `labels` on one device may be relied on, other than what follows from the above.
Results may differ from the reference program's by a relative error of at most 0.0033.
Values sent between devices are 32-bit elements; how exact they have to be, the bound alone decides.
No kernel may reach another device: no remote copies, remote signals or barrier semaphores. Data moves between devices by JAX's collectives and lax.ppermute only.
A program may use at most 64 MiB of HBM per device.

```python
import math
import jax
import jax.numpy as jnp
import numpy as np

FW = 128
BLOCKS = 8192
K = 8
ROWS_T = 128
TILES_DEV = 16
ITERS = 2
BLK_DEV = 2048
TILES = 128
ROWS = 16384
N_FEAT = 4


def draw_live_slots(key, part):
    tile_ids = jnp.arange(TILES, dtype=jnp.int32)[:, None]
    shard_ids = tile_ids // TILES_DEV
    shard_total = TILES // TILES_DEV
    limits = jnp.maximum(1, K * (shard_ids + 1) // shard_total)
    drawn = jax.random.randint(key, (TILES, N_FEAT), 0, 1 << 20, dtype=jnp.int32)
    counts = 1 + drawn % limits
    return jnp.where(tile_ids == TILES - 1, K, counts).astype(jnp.int32)


def with_ends(values, rng, least, high):
    extent = values.shape
    place = [jax.random.randint(jax.random.fold_in(rng, axis), (), 0, extent[axis]) for axis in range(len(extent))]
    values = values.at[tuple(place)].set(least)
    longest = extent.index(max(extent))
    place[longest] = (place[longest] + 1) % extent[longest]
    return values.at[tuple(place)].set(high)


def shard_levels(own_key, shape, cuts, least, top_value):
    loudness = 1.0
    for dim, shards_of in cuts:
        draws = jax.random.uniform(jax.random.fold_in(jax.random.fold_in(own_key, 6), dim), (shards_of,), jnp.float32, least / len(cuts), top_value / len(cuts))
        loudness = loudness * jnp.repeat(jnp.exp(draws), shape[dim] // shards_of).reshape((-1,) + (1,) * (len(shape) - 1 - dim))
    return loudness


def rank_table(amount, slope):
    weights = [(1 << 20) // math.isqrt(standing ** slope) + 1 for standing in range(1, amount + 1)]
    scale = 1 + sum(weights) // (1 << 30)
    return np.cumsum(np.array([max(1, weight // scale) for weight in weights]))


def ranked_ids(rng, shape, amount, skew):
    grid = rank_table(amount, skew)
    ticket = jax.random.randint(jax.random.fold_in(rng, 1), shape, 0, int(grid[amount - 1]))
    standing = jnp.searchsorted(jnp.asarray(grid, jnp.int32), ticket, side="right")
    return jax.random.permutation(jax.random.fold_in(rng, 2), amount)[standing].astype(jnp.int32)


def centred(key, dims, scale, most, cuts=(), kind=jnp.bfloat16):
    values = scale * jax.random.normal(key, dims, jnp.float32)
    if cuts:
        values = values * shard_levels(key, dims, cuts, -0.22, 0.18)
    return jnp.clip(values, -most, most).astype(kind)


def setup_inputs(seed: int = 0) -> dict:
    key_of = jax.random.split(jax.random.key(seed), 6)
    return {
        "values": centred(key_of[0], (TILES, N_FEAT * K, ROWS_T, FW), FW ** -0.5, 0.5, ((0, 8), (1, 4))),
        "columns": with_ends(ranked_ids(key_of[1], (TILES, N_FEAT * K), BLK_DEV, 2), jax.random.fold_in(key_of[1], 3), 0, BLK_DEV - 1).astype(jnp.int32),
        "live_slots": draw_live_slots(jax.random.fold_in(key_of[5], 71), 0),
        "labels": with_ends((jax.random.randint(key_of[3], (ROWS,), 0, 2) < 1).astype(jnp.int32), jax.random.fold_in(key_of[3], 1), 0, 1),
        "weights": centred(key_of[4], (BLOCKS, FW), 0.125, 0.75, ((0, 4),), jnp.float32),
    }


def group_mask(live_slots, group):
    slots = jnp.arange(K, dtype=jnp.int32)[None, :]
    return (slots < live_slots[:, group:group + 1]).astype(jnp.float32)


def forward_all(values, columns, live_slots, vector):
    total = jnp.zeros((ROWS,), jnp.float32)
    for group in range(N_FEAT):
        tiles = values[:, group * K:(group + 1) * K].astype(jnp.float32)
        index = group * BLK_DEV + columns[:, group * K:(group + 1) * K]
        picked = (vector[index] * group_mask(live_slots, group)[:, :, None]).astype(jnp.bfloat16).astype(jnp.float32)
        total = total + jnp.einsum("tjrf,tjf->tr", tiles, picked).reshape(-1)
    return total


def transpose_all(values, columns, live_slots, rows_term):
    rows_half = rows_term.astype(jnp.bfloat16).astype(jnp.float32).reshape(TILES, ROWS_T)
    pieces = []
    for group in range(N_FEAT):
        tiles = values[:, group * K:(group + 1) * K].astype(jnp.float32)
        contrib = jnp.einsum("tjrf,tr->tjf", tiles, rows_half) * group_mask(live_slots, group)[:, :, None]
        index = columns[:, group * K:(group + 1) * K].reshape(-1)
        pieces.append(jax.ops.segment_sum(contrib.reshape(-1, FW), index, num_segments=BLK_DEV))
    return jnp.concatenate(pieces, axis=0)


def reference(values, columns, live_slots, labels, weights):
    margin = forward_all(values, columns, live_slots, weights)
    prob = jax.nn.sigmoid(margin)
    curvature = prob * (1.0 - prob)
    gradient = weights + transpose_all(values, columns, live_slots, prob - labels.astype(jnp.float32))
    residual = -gradient
    direction = residual
    step_vector = jnp.zeros_like(weights)
    norm_now = jnp.sum(residual * residual)
    for turn_index in range(ITERS):
        along = forward_all(values, columns, live_slots, direction)
        image = direction + transpose_all(values, columns, live_slots, curvature * along)
        alpha = norm_now / jnp.sum(direction * image)
        step_vector = step_vector + alpha * direction
        residual = residual - alpha * image
        norm_next = jnp.sum(residual * residual)
        direction = residual + (norm_next / norm_now) * direction
        norm_now = norm_next
    return step_vector, gradient
```

```python
import jax
import jax.numpy as jnp
from jax import lax
from jax.sharding import PartitionSpec as P


def split_halves(array):
    high = array.astype(jnp.bfloat16)
    low = (array - high.astype(jnp.float32)).astype(jnp.bfloat16)
    return high, low


def pick_sum(onehot, array):
    high, low = split_halves(array)
    both = jnp.dot(
        onehot, jnp.concatenate([high, low], axis=1), preferred_element_type=jnp.float32
    )
    width = array.shape[1]
    return both[:, :width] + both[:, width:]


def swap(array, axis, distance):
    size = lax.axis_size(axis)
    return lax.ppermute(array, axis, [(i, i ^ distance) for i in range(size)])


def feat_parts(array):
    size = lax.axis_size("feat")
    return [array] + [
        lax.ppermute(array, "feat", [(i, (i + k) % size) for i in range(size)])
        for k in range(1, size)
    ]


def feat_sum(array):
    parts = feat_parts(array)
    total = parts[0]
    for part in parts[1:]:
        total = total + part
    return total


def inst_parts(array):
    size = lax.axis_size("inst")
    if size != 8:
        gathered = lax.all_gather(array, "inst", axis=0)
        return [gathered[i] for i in range(size)]
    parts = [array] + [swap(array, "inst", k) for k in (2, 4, 6)]
    return parts + [swap(part, "inst", 1) for part in parts]


def inst_sum(array):
    size = lax.axis_size("inst")
    distance = 1
    while distance < size:
        array = array + swap(array, "inst", distance)
        distance *= 2
    return array


def per_device(values, columns, live_slots, labels, weights):
    tiles, slots, rows, width = values.shape
    block_count = weights.shape[0]
    share = block_count // lax.axis_size("inst")
    offset = lax.axis_index("inst") * share
    live = lax.broadcasted_iota(jnp.int32, (tiles, slots), 1) < live_slots
    mask = live.astype(jnp.float32).reshape(-1, 1)
    own_ids = jnp.where(live, columns, -2).reshape(-1)
    sent_ids = jnp.where(live, columns, -1).reshape(1, -1).astype(jnp.float32)
    slot_count = tiles * slots

    def forward(picked):
        return jnp.einsum(
            "tjrf,tjf->tr",
            values,
            picked.astype(jnp.bfloat16).reshape(tiles, slots, width),
            preferred_element_type=jnp.float32,
        )

    def back(rows_term):
        out = jnp.einsum(
            "tjrf,tr->tjf",
            values,
            rows_term.astype(jnp.bfloat16),
            preferred_element_type=jnp.float32,
        )
        return out.reshape(slot_count, width) * mask

    def scalar_row(*scalars):
        lane = lax.broadcasted_iota(jnp.int32, (8, width), 1)
        row = jnp.zeros((8, width), jnp.float32)
        for place, scalar in enumerate(scalars):
            row = jnp.where(lane == place, scalar, row)
        return row

    weights_slot = weights[columns.reshape(-1)] * mask
    weights_share = lax.dynamic_slice_in_dim(weights, offset, share, 0)

    margin = feat_sum(forward(weights_slot))
    prob = jax.nn.sigmoid(margin)
    curvature = prob * (1.0 - prob)
    first = back(prob - labels.astype(jnp.float32).reshape(tiles, rows))

    ids_block = jnp.broadcast_to(sent_ids.reshape(-1, width), (8, width))
    parts = inst_parts(jnp.concatenate([first, ids_block], axis=0))
    all_ids = jnp.concatenate([p[slot_count] for p in parts]).astype(jnp.int32)
    wanted = jnp.concatenate([own_ids, offset + jnp.arange(share, dtype=jnp.int32)])
    onehot = (wanted[:, None] == all_ids[None, :]).astype(jnp.bfloat16)
    summed = pick_sum(onehot, jnp.concatenate([p[:slot_count] for p in parts], axis=0))
    start_slot = -(weights_slot + summed[:slot_count])
    gradient = weights_share + summed[slot_count:]
    start_share = -gradient

    along_part = forward(start_slot)
    total = feat_sum(
        jnp.concatenate([along_part, scalar_row(jnp.sum(gradient * gradient))], axis=0)
    )
    along = total[:tiles]
    norm_part = total[tiles, 0]
    curved = curvature * along
    second = back(curved)
    extra = scalar_row(norm_part, jnp.sum(curved * along))
    parts = inst_parts(jnp.concatenate([second, extra], axis=0))
    summed = pick_sum(onehot, jnp.concatenate([p[:slot_count] for p in parts], axis=0))
    scalars = sum(p[slot_count] for p in parts)
    norm_now = scalars[0]
    curve_now = scalars[1]
    alpha = norm_now / (norm_now + curve_now)
    next_slot = start_slot - alpha * (start_slot + summed[:slot_count])
    next_share = start_share - alpha * (start_share + summed[slot_count:])
    total = feat_sum(
        jnp.concatenate(
            [
                forward(next_slot),
                scalar_row(jnp.sum(next_share * next_share), jnp.sum(next_share * start_share)),
            ],
            axis=0,
        )
    )
    turn = total[:tiles]
    scalars = inst_sum(
        scalar_row(
            total[tiles, 0],
            total[tiles, 1],
            jnp.sum(curvature * turn * turn),
            jnp.sum(curvature * turn * along),
        )
    )
    norm_next, cross, turn_turn, turn_along = (scalars[0, i] for i in range(4))
    ratio = norm_next / norm_now
    bottom = (
        norm_next
        + 2.0 * ratio * cross
        + ratio * ratio * norm_now
        + turn_turn
        + 2.0 * ratio * turn_along
        + ratio * ratio * curve_now
    )
    alpha_next = norm_next / bottom
    step = alpha * start_share + alpha_next * (next_share + ratio * start_share)
    return (step, gradient)


def solution(mesh):
    in_specs = (
        P("inst", "feat", None, None),
        P("inst", "feat"),
        P("inst", "feat"),
        P("inst"),
        P("feat", None),
    )
    out_specs = (P(("feat", "inst"), None), P(("feat", "inst"), None))
    return jax.shard_map(
        per_device, mesh=mesh, in_specs=in_specs, out_specs=out_specs, check_vma=False
    )
```

```python
import functools

import jax
import jax.numpy as jnp
from jax import lax
from jax.experimental import pallas as pl
from jax.experimental.pallas import tpu as pltpu
from jax.sharding import PartitionSpec as P

F32 = jnp.float32
BF16 = jnp.bfloat16
SUB = 8
LIMIT = 24 * 1024 * 1024


def row_iota(shape):
    return lax.broadcasted_iota(jnp.int32, shape, 0)


def lane_iota(shape):
    return lax.broadcasted_iota(jnp.int32, shape, 1)


def total(array):
    return jnp.sum(jnp.sum(array, axis=0, keepdims=True), axis=1, keepdims=True)


def scalar_rows(width, *scalars):
    lane = lane_iota((SUB, width))
    block = jnp.zeros((SUB, width), F32)
    for place, scalar in enumerate(scalars):
        block = jnp.where(lane == place, scalar, block)
    return block


def read_scalar(block, place):
    lane = lane_iota(block.shape)
    return jnp.sum(jnp.where(lane == place, block, 0.0), axis=1, keepdims=True)


def forward_tile(tile, picked):
    slots, rows, width = tile.shape
    product = lax.dot_general(
        picked.astype(BF16),
        tile.reshape(slots * rows, width),
        (((1,), (1,)), ((), ())),
        preferred_element_type=F32,
    )
    mine = row_iota((slots, rows))
    kept = jnp.where(mine == 0, product[:, :rows], 0.0)
    for s in range(1, slots):
        kept = kept + jnp.where(mine == s, product[:, s * rows : (s + 1) * rows], 0.0)
    return jnp.sum(kept, axis=0, keepdims=True)


def back_tile(tile, rows_term):
    slots, rows, width = tile.shape
    mine = row_iota((slots, rows))
    spread = jnp.concatenate(
        [jnp.where(mine == s, rows_term, 0.0) for s in range(slots)], axis=1
    ).astype(BF16)
    return jnp.dot(spread, tile.reshape(slots * rows, width), preferred_element_type=F32)


def forward_all(values, picked, out):
    tiles, slots = values.shape[:2]
    for t in range(tiles):
        out[t : t + 1, :] = forward_tile(values[t], picked[t * slots : (t + 1) * slots, :])


def back_all(values, rows_term, ids, out):
    tiles, slots = values.shape[:2]
    for t in range(tiles):
        block = slice(t * slots, (t + 1) * slots)
        out[block, :] = jnp.where(
            ids[block, :] >= 0.0, back_tile(values[t], rows_term[t : t + 1, :]), 0.0
        )


def first_kernel(share, columns, live, weights, values_in, values, ids, picked, own, along,
                 weights_here, weights_sem, values_sem):
    tiles, slots, rows, width = values.shape
    whole = pltpu.make_async_copy(weights, weights_here, weights_sem)
    whole.start()
    loads = [
        pltpu.make_async_copy(values_in.at[t], values.at[t], values_sem.at[t])
        for t in range(tiles)
    ]
    for load in loads:
        load.start()
    whole.wait()
    for t in range(tiles):
        count = live[0, t]
        for j in range(slots):
            slot = t * slots + j
            column = columns[j, t]
            used = j < count
            row = weights_here[pl.ds(column, 1), :]
            picked[slot : slot + 1, :] = jnp.where(used, row, 0.0)
            ids[slot : slot + 1, :] = jnp.full(
                (1, width), jnp.where(used, column, -2), jnp.int32
            ).astype(F32)
    offset = pl.multiple_of(lax.axis_index("inst") * share, SUB)
    own[...] = weights_here[pl.ds(offset, share), :]
    for t in range(tiles):
        loads[t].wait()
        along[t : t + 1, :] = forward_tile(values[t], picked[t * slots : (t + 1) * slots, :])


def gradient_kernel(count, labels, values, ids, *refs):
    parts, (payload, curvature) = refs[:count], refs[count:]
    slots = ids.shape[0]
    margin = parts[0][...]
    for part in parts[1:]:
        margin = margin + part[...]
    prob = 1.0 / (1.0 + jnp.exp(-margin))
    curvature[...] = prob * (1.0 - prob)
    back_all(values, prob - labels[...].astype(F32), ids, payload)
    square = ids[...]
    diagonal = row_iota(square.shape) == lane_iota(square.shape)
    sent = jnp.sum(jnp.where(diagonal, square, 0.0), axis=0, keepdims=True)
    sent = jnp.where(sent < 0.0, -1.0, sent)
    payload[slots:, :] = jnp.broadcast_to(sent, (SUB, sent.shape[1]))


def stack_halves(parts, slots, halves):
    width = parts[0].shape[1]
    for k, part in enumerate(parts):
        block = part[:slots, :]
        high = block.astype(BF16)
        halves[k * slots : (k + 1) * slots, :width] = high
        halves[k * slots : (k + 1) * slots, width:] = (block - high.astype(F32)).astype(BF16)


def pick_sums(onehot, halves):
    both = jnp.dot(onehot[...], halves[...], preferred_element_type=F32)
    width = both.shape[1] // 2
    return both[:, :width] + both[:, width:]


def start_kernel(count, values, ids, picked, own, *refs):
    parts = refs[:count]
    gradient, start_slot, onehot, payload, halves = refs[count:]
    tiles = values.shape[0]
    slots, width = ids.shape
    share = own.shape[0]
    offset = lax.axis_index("inst") * share
    blocks = (row_iota((share, width)) + offset).astype(F32)
    for k, part in enumerate(parts):
        sent = part[slots : slots + 1, :]
        place = slice(k * slots, (k + 1) * slots)
        onehot[:slots, place] = jnp.where(ids[...] == sent, 1.0, 0.0).astype(BF16)
        onehot[slots:, place] = jnp.where(blocks == sent, 1.0, 0.0).astype(BF16)
    stack_halves(parts, slots, halves)
    summed = pick_sums(onehot, halves)
    start_slot[...] = -(picked[...] + summed[:slots, :])
    forward_all(values, start_slot, payload)
    slope = own[...] + summed[slots:, :]
    gradient[...] = slope
    payload[tiles:, :] = scalar_rows(width, total(slope * slope))


def curve_kernel(count, values, ids, curvature, *refs):
    parts, (along, payload) = refs[:count], refs[count:]
    tiles = values.shape[0]
    slots, width = ids.shape
    summed = parts[0][...]
    for part in parts[1:]:
        summed = summed + part[...]
    here = summed[:tiles, :]
    along[...] = here
    curved = curvature[...] * here
    back_all(values, curved, ids, payload)
    rounded = curved.astype(BF16).astype(F32)
    norm_part = summed[tiles : tiles + 1, 0:1]
    payload[slots:, :] = scalar_rows(width, norm_part, total(rounded * here))


def turn_kernel(count, values, onehot, start_slot, gradient, *refs):
    parts = refs[:count]
    next_share, known, payload, halves, next_slot = refs[count:]
    tiles = values.shape[0]
    slots, width = start_slot.shape
    scalars = parts[0][slots:, :]
    for part in parts[1:]:
        scalars = scalars + part[slots:, :]
    norm_now = read_scalar(scalars[0:1, :], 0)
    curve_now = read_scalar(scalars[0:1, :], 1)
    alpha = norm_now / (norm_now + curve_now)
    stack_halves(parts, slots, halves)
    summed = pick_sums(onehot, halves)
    start = start_slot[...]
    next_slot[...] = start - alpha * (start + summed[:slots, :])
    forward_all(values, next_slot, payload)
    start_own = -gradient[...]
    turned = start_own - alpha * (start_own + summed[slots:, :])
    next_share[...] = turned
    payload[tiles:, :] = scalar_rows(width, total(turned * turned), total(turned * start_own))
    known[...] = scalar_rows(width, norm_now, curve_now, alpha)


def inner_kernel(count, curvature, along, *refs):
    parts, (scalars,) = refs[:count], refs[count:]
    tiles, width = along.shape
    summed = parts[0][...]
    for part in parts[1:]:
        summed = summed + part[...]
    turn = summed[:tiles, :]
    bent = curvature[...] * turn
    scalars[...] = scalar_rows(
        width,
        summed[tiles : tiles + 1, 0:1],
        summed[tiles : tiles + 1, 1:2],
        total(bent * turn),
        total(bent * along[...]),
    )


def last_kernel(scalars, known, gradient, next_share, step):
    row = scalars[0:1, :]
    norm_next, cross, turn_turn, turn_along = (read_scalar(row, i) for i in range(4))
    row = known[0:1, :]
    norm_now, curve_now, alpha = (read_scalar(row, i) for i in range(3))
    ratio = norm_next / norm_now
    bottom = (
        norm_next
        + turn_turn
        + 2.0 * ratio * (cross + turn_along)
        + ratio * ratio * (norm_now + curve_now)
    )
    alpha_next = norm_next / bottom
    start = -gradient[...]
    step[...] = alpha * start + alpha_next * (next_share[...] + ratio * start)


def near(shape, dtype=F32):
    return pltpu.VMEM(shape, dtype)


def call(kernel, out_shape, args, in_specs=None, scratch_shapes=(), keep=None):
    vmem = pl.BlockSpec(memory_space=pltpu.VMEM)
    if in_specs is None:
        in_specs = [vmem] * len(args)
        args = [pltpu.with_memory_space_constraint(a, pltpu.VMEM) for a in args]
    return pl.pallas_call(
        kernel,
        out_shape=out_shape,
        in_specs=in_specs,
        out_specs=jax.tree.map(lambda _: vmem, out_shape),
        scratch_shapes=list(scratch_shapes),
        compiler_params=pltpu.CompilerParams(vmem_limit_bytes=LIMIT),
    )(*args)


def swap(array, axis, distance):
    size = lax.axis_size(axis)
    return lax.ppermute(array, axis, [(i, i ^ distance) for i in range(size)])


def feat_parts(array):
    size = lax.axis_size("feat")
    return [array] + [
        lax.ppermute(array, "feat", [(i, (i + k) % size) for i in range(size)])
        for k in range(1, size)
    ]


def inst_parts(array):
    size = lax.axis_size("inst")
    if size != 8:
        gathered = lax.all_gather(array, "inst", axis=0)
        return [gathered[i] for i in range(size)]
    parts = [array] + [swap(array, "inst", k) for k in (2, 4, 6)]
    return parts + [swap(part, "inst", 1) for part in parts]


def inst_sum(array):
    size = lax.axis_size("inst")
    distance = 1
    while distance < size:
        array = array + swap(array, "inst", distance)
        distance *= 2
    return array


def per_device(values, columns, live_slots, labels, weights):
    tiles, slots_of, rows, width = values.shape
    slots = tiles * slots_of
    share = weights.shape[0] // lax.axis_size("inst")
    feats, insts = lax.axis_size("feat"), lax.axis_size("inst")
    smem = pl.BlockSpec(memory_space=pltpu.SMEM)
    hbm = pl.BlockSpec(memory_space=pl.ANY)

    values_here, ids, picked, own, part = call(
        functools.partial(first_kernel, share),
        (
            near(values.shape, BF16),
            near((slots, width)),
            near((slots, width)),
            near((share, width)),
            near((tiles, rows)),
        ),
        (columns.T, live_slots.T, weights, values),
        in_specs=[smem, smem, hbm, hbm],
        scratch_shapes=[
            pltpu.VMEM(weights.shape, F32),
            pltpu.SemaphoreType.DMA,
            pltpu.SemaphoreType.DMA((tiles,)),
        ],
    )
    payload, curvature = call(
        functools.partial(gradient_kernel, feats),
        (near((slots + SUB, width)), near((tiles, rows))),
        (labels.reshape(tiles, rows), values_here, ids, *feat_parts(part)),
    )
    halves = pltpu.VMEM((insts * slots, 2 * width), BF16)
    gradient, start_slot, onehot, payload = call(
        functools.partial(start_kernel, insts),
        (
            near((share, width)),
            near((slots, width)),
            near((slots + share, insts * slots), BF16),
            near((tiles + SUB, rows)),
        ),
        (values_here, ids, picked, own, *inst_parts(payload)),
        scratch_shapes=[halves],
    )
    along, payload = call(
        functools.partial(curve_kernel, feats),
        (near((tiles, rows)), near((slots + SUB, width))),
        (values_here, ids, curvature, *feat_parts(payload)),
    )
    next_share, known, payload = call(
        functools.partial(turn_kernel, insts),
        (near((share, width)), near((SUB, width)), near((tiles + SUB, rows))),
        (values_here, onehot, start_slot, gradient, *inst_parts(payload)),
        scratch_shapes=[halves, pltpu.VMEM((slots, width), F32)],
    )
    scalars = call(
        functools.partial(inner_kernel, feats),
        near((SUB, width)),
        (curvature, along, *feat_parts(payload)),
    )
    step = call(
        last_kernel,
        near((share, width)),
        (inst_sum(scalars), known, gradient, next_share),
    )
    return (step, gradient)


def solution(mesh):
    in_specs = (
        P("inst", "feat", None, None),
        P("inst", "feat"),
        P("inst", "feat"),
        P("inst"),
        P("feat", None),
    )
    out_specs = (P(("feat", "inst"), None), P(("feat", "inst"), None))
    return jax.shard_map(
        per_device, mesh=mesh, in_specs=in_specs, out_specs=out_specs, check_vma=False
    )
```

```python
import functools

import jax
import jax.numpy as jnp
from jax import lax
from jax.experimental import pallas as pl
from jax.experimental.pallas import tpu as pltpu
from jax.sharding import PartitionSpec as P

F32 = jnp.float32
BF16 = jnp.bfloat16
SUB = 8
LIMIT = 24 * 1024 * 1024


def row_iota(shape):
    return lax.broadcasted_iota(jnp.int32, shape, 0)


def lane_iota(shape):
    return lax.broadcasted_iota(jnp.int32, shape, 1)


def total(array):
    return jnp.sum(jnp.sum(array, axis=0, keepdims=True), axis=1, keepdims=True)


def scalar_rows(width, *scalars):
    lane = lane_iota((SUB, width))
    block = jnp.zeros((SUB, width), F32)
    for place, scalar in enumerate(scalars):
        block = jnp.where(lane == place, scalar, block)
    return block


def read_scalar(block, place):
    lane = lane_iota(block.shape)
    return jnp.sum(jnp.where(lane == place, block, 0.0), axis=1, keepdims=True)


def forward_tile(tile, picked):
    slots, rows, width = tile.shape
    product = lax.dot_general(
        picked.astype(BF16),
        tile.reshape(slots * rows, width),
        (((1,), (1,)), ((), ())),
        preferred_element_type=F32,
    )
    mine = row_iota((slots, rows))
    kept = jnp.where(mine == 0, product[:, :rows], 0.0)
    for s in range(1, slots):
        kept = kept + jnp.where(mine == s, product[:, s * rows : (s + 1) * rows], 0.0)
    return jnp.sum(kept, axis=0, keepdims=True)


def back_tile(tile, rows_term):
    slots, rows, width = tile.shape
    mine = row_iota((slots, rows))
    spread = jnp.concatenate(
        [jnp.where(mine == s, rows_term, 0.0) for s in range(slots)], axis=1
    ).astype(BF16)
    return jnp.dot(spread, tile.reshape(slots * rows, width), preferred_element_type=F32)


def forward_all(values, picked, out):
    tiles, slots = values.shape[:2]
    for t in range(tiles):
        out[t : t + 1, :] = forward_tile(values[t], picked[t * slots : (t + 1) * slots, :])


def back_all(values, rows_term, ids, out):
    tiles, slots = values.shape[:2]
    for t in range(tiles):
        block = slice(t * slots, (t + 1) * slots)
        out[block, :] = jnp.where(
            ids[block, :] >= 0.0, back_tile(values[t], rows_term[t : t + 1, :]), 0.0
        )


def first_kernel(share, columns_in, live_in, weights, values_in, values, ids, picked, own, along,
                 columns, live, weights_here, small_sem, values_sem):
    tiles, slots, rows, width = values.shape
    smalls = [
        pltpu.make_async_copy(columns_in, columns, small_sem.at[0]),
        pltpu.make_async_copy(live_in, live, small_sem.at[1]),
        pltpu.make_async_copy(weights, weights_here, small_sem.at[2]),
    ]
    for small in smalls:
        small.start()
    loads = [
        pltpu.make_async_copy(values_in.at[t], values.at[t], values_sem.at[t])
        for t in range(tiles)
    ]
    for load in loads:
        load.start()
    for small in smalls:
        small.wait()
    for t in range(tiles):
        count = live[0, t]
        for j in range(slots):
            slot = t * slots + j
            column = columns[j, t]
            used = j < count
            row = weights_here[pl.ds(column, 1), :]
            picked[slot : slot + 1, :] = jnp.where(used, row, 0.0)
            ids[slot : slot + 1, :] = jnp.full(
                (1, width), jnp.where(used, column, -2), jnp.int32
            ).astype(F32)
    offset = pl.multiple_of(lax.axis_index("inst") * share, SUB)
    own[...] = weights_here[pl.ds(offset, share), :]
    for t in range(tiles):
        loads[t].wait()
        along[t : t + 1, :] = forward_tile(values[t], picked[t * slots : (t + 1) * slots, :])


def gradient_kernel(count, labels, values, ids, *refs):
    parts, (payload, curvature) = refs[:count], refs[count:]
    slots = ids.shape[0]
    margin = parts[0][...]
    for part in parts[1:]:
        margin = margin + part[...]
    prob = 1.0 / (1.0 + jnp.exp(-margin))
    curvature[...] = prob * (1.0 - prob)
    back_all(values, prob - labels[...].astype(F32), ids, payload)
    square = ids[...]
    diagonal = row_iota(square.shape) == lane_iota(square.shape)
    sent = jnp.sum(jnp.where(diagonal, square, 0.0), axis=0, keepdims=True)
    sent = jnp.where(sent < 0.0, -1.0, sent)
    payload[slots:, :] = jnp.broadcast_to(sent, (SUB, sent.shape[1]))


def stack_halves(parts, slots, halves):
    width = parts[0].shape[1]
    for k, part in enumerate(parts):
        block = part[:slots, :]
        high = block.astype(BF16)
        halves[k * slots : (k + 1) * slots, :width] = high
        halves[k * slots : (k + 1) * slots, width:] = (block - high.astype(F32)).astype(BF16)


def pick_sums(onehot, halves):
    both = jnp.dot(onehot[...], halves[...], preferred_element_type=F32)
    width = both.shape[1] // 2
    return both[:, :width] + both[:, width:]


def start_kernel(count, values, ids, picked, own, *refs):
    parts = refs[:count]
    gradient, start_slot, onehot, payload, halves = refs[count:]
    tiles = values.shape[0]
    slots, width = ids.shape
    share = own.shape[0]
    offset = lax.axis_index("inst") * share
    blocks = (row_iota((share, width)) + offset).astype(F32)
    for k, part in enumerate(parts):
        sent = part[slots : slots + 1, :]
        place = slice(k * slots, (k + 1) * slots)
        onehot[:slots, place] = jnp.where(ids[...] == sent, 1.0, 0.0).astype(BF16)
        onehot[slots:, place] = jnp.where(blocks == sent, 1.0, 0.0).astype(BF16)
    stack_halves(parts, slots, halves)
    summed = pick_sums(onehot, halves)
    start_slot[...] = -(picked[...] + summed[:slots, :])
    forward_all(values, start_slot, payload)
    slope = own[...] + summed[slots:, :]
    gradient[...] = slope
    payload[tiles:, :] = scalar_rows(width, total(slope * slope))


def curve_kernel(count, values, ids, curvature, *refs):
    parts, (along, payload) = refs[:count], refs[count:]
    tiles = values.shape[0]
    slots, width = ids.shape
    summed = parts[0][...]
    for part in parts[1:]:
        summed = summed + part[...]
    here = summed[:tiles, :]
    along[...] = here
    curved = curvature[...] * here
    back_all(values, curved, ids, payload)
    rounded = curved.astype(BF16).astype(F32)
    norm_part = summed[tiles : tiles + 1, 0:1]
    payload[slots:, :] = scalar_rows(width, norm_part, total(rounded * here))


def turn_kernel(count, values, onehot, start_slot, gradient, *refs):
    parts = refs[:count]
    next_share, known, payload, halves, next_slot = refs[count:]
    tiles = values.shape[0]
    slots, width = start_slot.shape
    scalars = parts[0][slots:, :]
    for part in parts[1:]:
        scalars = scalars + part[slots:, :]
    norm_now = read_scalar(scalars[0:1, :], 0)
    curve_now = read_scalar(scalars[0:1, :], 1)
    alpha = norm_now / (norm_now + curve_now)
    stack_halves(parts, slots, halves)
    summed = pick_sums(onehot, halves)
    start = start_slot[...]
    next_slot[...] = start - alpha * (start + summed[:slots, :])
    forward_all(values, next_slot, payload)
    start_own = -gradient[...]
    turned = start_own - alpha * (start_own + summed[slots:, :])
    next_share[...] = turned
    payload[tiles:, :] = scalar_rows(width, total(turned * turned), total(turned * start_own))
    known[...] = scalar_rows(width, norm_now, curve_now, alpha)


def inner_kernel(count, curvature, along, *refs):
    parts, (scalars, first_only) = refs[:count], refs[count:]
    tiles, width = along.shape
    summed = parts[0][...]
    for part in parts[1:]:
        summed = summed + part[...]
    turn = summed[:tiles, :]
    bent = curvature[...] * turn
    block = scalar_rows(
        width,
        summed[tiles : tiles + 1, 0:1],
        summed[tiles : tiles + 1, 1:2],
        total(bent * turn),
        total(bent * along[...]),
    )
    scalars[...] = block
    first_only[...] = jnp.where(lax.axis_index("feat") == 0, block, 0.0)


def last_kernel(known, gradient, next_share, *refs):
    parts, step = refs[:-1], refs[-1]
    row = parts[0][0:1, :]
    for part in parts[1:]:
        row = row + part[0:1, :]
    norm_next, cross, turn_turn, turn_along = (read_scalar(row, i) for i in range(4))
    row = known[0:1, :]
    norm_now, curve_now, alpha = (read_scalar(row, i) for i in range(3))
    ratio = norm_next / norm_now
    bottom = (
        norm_next
        + turn_turn
        + 2.0 * ratio * (cross + turn_along)
        + ratio * ratio * (norm_now + curve_now)
    )
    alpha_next = norm_next / bottom
    start = -gradient[...]
    step[...] = alpha * start + alpha_next * (next_share[...] + ratio * start)


def near(shape, dtype=F32):
    return pltpu.VMEM(shape, dtype)


def call(kernel, out_shape, args, in_specs=None, scratch_shapes=()):
    vmem = pl.BlockSpec(memory_space=pltpu.VMEM)
    if in_specs is None:
        in_specs = [vmem] * len(args)
        args = [pltpu.with_memory_space_constraint(a, pltpu.VMEM) for a in args]
    return pl.pallas_call(
        kernel,
        out_shape=out_shape,
        in_specs=in_specs,
        out_specs=jax.tree.map(lambda _: vmem, out_shape),
        scratch_shapes=list(scratch_shapes),
        compiler_params=pltpu.CompilerParams(vmem_limit_bytes=LIMIT),
    )(*args)


def swap(array, axis, distance):
    size = lax.axis_size(axis)
    return lax.ppermute(array, axis, [(i, i ^ distance) for i in range(size)])


def feat_parts(array):
    size = lax.axis_size("feat")
    return [array] + [
        lax.ppermute(array, "feat", [(i, (i + k) % size) for i in range(size)])
        for k in range(1, size)
    ]


def inst_parts(array):
    size = lax.axis_size("inst")
    if size != 8:
        gathered = lax.all_gather(array, "inst", axis=0)
        return [gathered[i] for i in range(size)]
    parts = [array] + [swap(array, "inst", k) for k in (2, 4, 6)]
    return parts + [swap(part, "inst", 1) for part in parts]


def inst_sum(array, first_only):
    size, feats = lax.axis_size("inst"), lax.axis_size("feat")
    if size == 2 * feats:
        fetched = first_only
        for low in (0, 1):
            pairs = [
                (i * feats + f, (i ^ (2 * f + low)) * feats + f)
                for i in range(size)
                for f in range(feats)
                if 2 * f + low
            ]
            fetched = fetched + lax.ppermute(array, ("inst", "feat"), pairs)
        return feat_parts(fetched)
    distance = 1
    while distance < size:
        array = array + swap(array, "inst", distance)
        distance *= 2
    return [array]


def per_device(values, columns, live_slots, labels, weights):
    tiles, slots_of, rows, width = values.shape
    slots = tiles * slots_of
    share = weights.shape[0] // lax.axis_size("inst")
    feats, insts = lax.axis_size("feat"), lax.axis_size("inst")

    values_here, ids, picked, own, part = call(
        functools.partial(first_kernel, share),
        (
            near(values.shape, BF16),
            near((slots, width)),
            near((slots, width)),
            near((share, width)),
            near((tiles, rows)),
        ),
        [
            pltpu.with_memory_space_constraint(a, pltpu.HBM)
            for a in (columns.T, live_slots.T, weights, values)
        ],
        in_specs=[pl.BlockSpec(memory_space=pltpu.HBM)] * 4,
        scratch_shapes=[
            pltpu.SMEM((slots_of, tiles), jnp.int32),
            pltpu.SMEM((1, tiles), jnp.int32),
            pltpu.VMEM(weights.shape, F32),
            pltpu.SemaphoreType.DMA((3,)),
            pltpu.SemaphoreType.DMA((tiles,)),
        ],
    )
    payload, curvature = call(
        functools.partial(gradient_kernel, feats),
        (near((slots + SUB, width)), near((tiles, rows))),
        (labels.reshape(tiles, rows), values_here, ids, *feat_parts(part)),
    )
    halves = pltpu.VMEM((insts * slots, 2 * width), BF16)
    gradient, start_slot, onehot, payload = call(
        functools.partial(start_kernel, insts),
        (
            near((share, width)),
            near((slots, width)),
            near((slots + share, insts * slots), BF16),
            near((tiles + SUB, rows)),
        ),
        (values_here, ids, picked, own, *inst_parts(payload)),
        scratch_shapes=[halves],
    )
    along, payload = call(
        functools.partial(curve_kernel, feats),
        (near((tiles, rows)), near((slots + SUB, width))),
        (values_here, ids, curvature, *feat_parts(payload)),
    )
    next_share, known, payload = call(
        functools.partial(turn_kernel, insts),
        (near((share, width)), near((SUB, width)), near((tiles + SUB, rows))),
        (values_here, onehot, start_slot, gradient, *inst_parts(payload)),
        scratch_shapes=[halves, pltpu.VMEM((slots, width), F32)],
    )
    scalars, first_only = call(
        functools.partial(inner_kernel, feats),
        (near((SUB, width)), near((SUB, width))),
        (curvature, along, *feat_parts(payload)),
    )
    step = call(
        last_kernel,
        near((share, width)),
        (known, gradient, next_share, *inst_sum(scalars, first_only)),
    )
    return (step, gradient)


def solution(mesh):
    in_specs = (
        P("inst", "feat", None, None),
        P("inst", "feat"),
        P("inst", "feat"),
        P("inst"),
        P("feat", None),
    )
    out_specs = (P(("feat", "inst"), None), P(("feat", "inst"), None))
    return jax.shard_map(
        per_device, mesh=mesh, in_specs=in_specs, out_specs=out_specs, check_vma=False
    )
```

```python
import functools

import jax
import jax.numpy as jnp
from jax import lax
from jax.experimental import pallas as pl
from jax.experimental.pallas import tpu as pltpu
from jax.sharding import PartitionSpec as P

F32 = jnp.float32
BF16 = jnp.bfloat16
SUB = 8
LIMIT = 24 * 1024 * 1024


def row_iota(shape):
    return lax.broadcasted_iota(jnp.int32, shape, 0)


def lane_iota(shape):
    return lax.broadcasted_iota(jnp.int32, shape, 1)


def total(array):
    return jnp.sum(jnp.sum(array, axis=0, keepdims=True), axis=1, keepdims=True)


def scalar_rows(width, *scalars):
    lane = lane_iota((SUB, width))
    block = jnp.zeros((SUB, width), F32)
    for place, scalar in enumerate(scalars):
        block = jnp.where(lane == place, scalar, block)
    return block


def read_scalar(block, place):
    lane = lane_iota(block.shape)
    return jnp.sum(jnp.where(lane == place, block, 0.0), axis=1, keepdims=True)


def forward_tile(tile, picked):
    slots, rows, width = tile.shape
    product = lax.dot_general(
        picked.astype(BF16),
        tile.reshape(slots * rows, width),
        (((1,), (1,)), ((), ())),
        preferred_element_type=F32,
    )
    mine = row_iota((slots, rows))
    kept = jnp.where(mine == 0, product[:, :rows], 0.0)
    for s in range(1, slots):
        kept = kept + jnp.where(mine == s, product[:, s * rows : (s + 1) * rows], 0.0)
    return jnp.sum(kept, axis=0, keepdims=True)


def back_tile(tile, rows_term):
    slots, rows, width = tile.shape
    mine = row_iota((slots, rows))
    spread = jnp.concatenate(
        [jnp.where(mine == s, rows_term, 0.0) for s in range(slots)], axis=1
    ).astype(BF16)
    return jnp.dot(spread, tile.reshape(slots * rows, width), preferred_element_type=F32)


def forward_all(values, picked, out):
    tiles, slots = values.shape[:2]
    for t in range(tiles):
        out[t : t + 1, :] = forward_tile(values[t], picked[t * slots : (t + 1) * slots, :])


def back_all(values, rows_term, ids, out):
    tiles, slots = values.shape[:2]
    for t in range(tiles):
        block = slice(t * slots, (t + 1) * slots)
        out[block, :] = jnp.where(
            ids[block, :] >= 0.0, back_tile(values[t], rows_term[t : t + 1, :]), 0.0
        )


def first_kernel(share, columns_in, live_in, weights, values_in, values, ids, picked, own, along,
                 columns, live, weights_here, small_sem, values_sem):
    tiles, slots, rows, width = values.shape
    smalls = [
        pltpu.make_async_copy(columns_in, columns, small_sem.at[0]),
        pltpu.make_async_copy(live_in, live, small_sem.at[1]),
        pltpu.make_async_copy(weights, weights_here, small_sem.at[2]),
    ]
    for small in smalls:
        small.start()
    load = pltpu.make_async_copy(values_in, values, values_sem)
    load.start()
    for small in smalls:
        small.wait()
    for t in range(tiles):
        count = live[0, t]
        for j in range(slots):
            slot = t * slots + j
            column = columns[j, t]
            used = j < count
            row = weights_here[pl.ds(column, 1), :]
            picked[slot : slot + 1, :] = jnp.where(used, row, 0.0)
            ids[slot : slot + 1, :] = jnp.full(
                (1, width), jnp.where(used, column, -2), jnp.int32
            ).astype(F32)
    offset = pl.multiple_of(lax.axis_index("inst") * share, SUB)
    own[...] = weights_here[pl.ds(offset, share), :]
    load.wait()
    forward_all(values, picked, along)


def gradient_kernel(count, labels, values, ids, *refs):
    parts, (payload, curvature) = refs[:count], refs[count:]
    slots = ids.shape[0]
    margin = parts[0][...]
    for part in parts[1:]:
        margin = margin + part[...]
    prob = 1.0 / (1.0 + jnp.exp(-margin))
    curvature[...] = prob * (1.0 - prob)
    back_all(values, prob - labels[...].astype(F32), ids, payload)
    square = ids[...]
    diagonal = row_iota(square.shape) == lane_iota(square.shape)
    sent = jnp.sum(jnp.where(diagonal, square, 0.0), axis=0, keepdims=True)
    sent = jnp.where(sent < 0.0, -1.0, sent)
    payload[slots:, :] = jnp.broadcast_to(sent, (SUB, sent.shape[1]))


def stack_halves(parts, slots, halves):
    width = parts[0].shape[1]
    for k, part in enumerate(parts):
        block = part[:slots, :]
        high = block.astype(BF16)
        halves[k * slots : (k + 1) * slots, :width] = high
        halves[k * slots : (k + 1) * slots, width:] = (block - high.astype(F32)).astype(BF16)


def pick_sums(onehot, halves):
    both = jnp.dot(onehot[...], halves[...], preferred_element_type=F32)
    width = both.shape[1] // 2
    return both[:, :width] + both[:, width:]


def start_kernel(count, values, ids, picked, own, *refs):
    parts = refs[:count]
    gradient, start_slot, onehot, payload, halves = refs[count:]
    tiles = values.shape[0]
    slots, width = ids.shape
    share = own.shape[0]
    offset = lax.axis_index("inst") * share
    blocks = (row_iota((share, width)) + offset).astype(F32)
    for k, part in enumerate(parts):
        sent = part[slots : slots + 1, :]
        place = slice(k * slots, (k + 1) * slots)
        onehot[:slots, place] = jnp.where(ids[...] == sent, 1.0, 0.0).astype(BF16)
        onehot[slots:, place] = jnp.where(blocks == sent, 1.0, 0.0).astype(BF16)
    stack_halves(parts, slots, halves)
    summed = pick_sums(onehot, halves)
    start_slot[...] = -(picked[...] + summed[:slots, :])
    forward_all(values, start_slot, payload)
    slope = own[...] + summed[slots:, :]
    gradient[...] = slope
    payload[tiles:, :] = scalar_rows(width, total(slope * slope))


def curve_kernel(count, values, ids, curvature, *refs):
    parts, (along, payload) = refs[:count], refs[count:]
    tiles = values.shape[0]
    slots, width = ids.shape
    summed = parts[0][...]
    for part in parts[1:]:
        summed = summed + part[...]
    here = summed[:tiles, :]
    along[...] = here
    curved = curvature[...] * here
    back_all(values, curved, ids, payload)
    rounded = curved.astype(BF16).astype(F32)
    norm_part = summed[tiles : tiles + 1, 0:1]
    payload[slots:, :] = scalar_rows(width, norm_part, total(rounded * here))


def turn_kernel(count, values, onehot, start_slot, gradient, *refs):
    parts = refs[:count]
    next_share, known, payload, halves, next_slot = refs[count:]
    tiles = values.shape[0]
    slots, width = start_slot.shape
    scalars = parts[0][slots:, :]
    for part in parts[1:]:
        scalars = scalars + part[slots:, :]
    norm_now = read_scalar(scalars[0:1, :], 0)
    curve_now = read_scalar(scalars[0:1, :], 1)
    alpha = norm_now / (norm_now + curve_now)
    stack_halves(parts, slots, halves)
    summed = pick_sums(onehot, halves)
    start = start_slot[...]
    next_slot[...] = start - alpha * (start + summed[:slots, :])
    forward_all(values, next_slot, payload)
    start_own = -gradient[...]
    turned = start_own - alpha * (start_own + summed[slots:, :])
    next_share[...] = turned
    payload[tiles:, :] = scalar_rows(width, total(turned * turned), total(turned * start_own))
    known[...] = scalar_rows(width, norm_now, curve_now, alpha)


def inner_kernel(count, curvature, along, *refs):
    parts, (scalars,) = refs[:count], refs[count:]
    tiles, width = along.shape
    summed = parts[0][...]
    for part in parts[1:]:
        summed = summed + part[...]
    turn = summed[:tiles, :]
    bent = curvature[...] * turn
    scalars[...] = scalar_rows(
        width,
        summed[tiles : tiles + 1, 0:1],
        summed[tiles : tiles + 1, 1:2],
        total(bent * turn),
        total(bent * along[...]),
    )


def last_kernel(known, gradient, next_share, *refs):
    parts, step = refs[:-1], refs[-1]
    row = parts[0][0:1, :]
    for part in parts[1:]:
        row = row + part[0:1, :]
    norm_next, cross, turn_turn, turn_along = (read_scalar(row, i) for i in range(4))
    row = known[0:1, :]
    norm_now, curve_now, alpha = (read_scalar(row, i) for i in range(3))
    ratio = norm_next / norm_now
    bottom = (
        norm_next
        + turn_turn
        + 2.0 * ratio * (cross + turn_along)
        + ratio * ratio * (norm_now + curve_now)
    )
    alpha_next = norm_next / bottom
    start = -gradient[...]
    step[...] = alpha * start + alpha_next * (next_share[...] + ratio * start)


def near(shape, dtype=F32):
    return pltpu.VMEM(shape, dtype)


def call(kernel, out_shape, args, in_specs=None, scratch_shapes=()):
    vmem = pl.BlockSpec(memory_space=pltpu.VMEM)
    if in_specs is None:
        in_specs = [vmem] * len(args)
        args = [pltpu.with_memory_space_constraint(a, pltpu.VMEM) for a in args]
    return pl.pallas_call(
        kernel,
        out_shape=out_shape,
        in_specs=in_specs,
        out_specs=jax.tree.map(lambda _: vmem, out_shape),
        scratch_shapes=list(scratch_shapes),
        compiler_params=pltpu.CompilerParams(vmem_limit_bytes=LIMIT),
    )(*args)


def swap(array, axis, distance):
    size = lax.axis_size(axis)
    return lax.ppermute(array, axis, [(i, i ^ distance) for i in range(size)])


def swap_both(array, distance):
    size, feats = lax.axis_size("inst"), lax.axis_size("feat")
    pairs = [
        (i * feats + f, (i ^ distance) * feats + (f ^ 1))
        for i in range(size)
        for f in range(feats)
    ]
    return lax.ppermute(array, ("inst", "feat"), pairs)


def feat_parts(array):
    distance = 1
    parts = [array]
    while distance < lax.axis_size("feat"):
        array = sum(parts[1:], parts[0])
        parts = [array, swap(array, "feat", distance | 1)]
        distance *= 2
    return parts


def inst_parts(array):
    size = lax.axis_size("inst")
    if size != 8:
        gathered = lax.all_gather(array, "inst", axis=0)
        return [gathered[i] for i in range(size)]
    parts = {0: array}
    for distance in (6, 4, 2, 1, 3):
        parts[distance] = swap(array, "inst", distance)
    for distance in (4, 6):
        parts[distance ^ 1] = swap(parts[distance], "inst", 1)
    return list(parts.values())


def inst_sum_parts(array):
    size = lax.axis_size("inst")
    stages = [(2, 4, 6), (1,)] if size == 8 else [(1 << b,) for b in range(size.bit_length() - 1)]
    parts = [array]
    for stage in stages:
        array = sum(parts[1:], parts[0])
        parts = [array] + [swap_both(array, distance) for distance in stage]
    return parts


def per_device(values, columns, live_slots, labels, weights):
    tiles, slots_of, rows, width = values.shape
    slots = tiles * slots_of
    share = weights.shape[0] // lax.axis_size("inst")
    insts, pair = lax.axis_size("inst"), 2

    values_here, ids, picked, own, part = call(
        functools.partial(first_kernel, share),
        (
            near(values.shape, BF16),
            near((slots, width)),
            near((slots, width)),
            near((share, width)),
            near((tiles, rows)),
        ),
        [
            pltpu.with_memory_space_constraint(a, pltpu.HBM)
            for a in (columns.T, live_slots.T, weights, values)
        ],
        in_specs=[pl.BlockSpec(memory_space=pltpu.HBM)] * 4,
        scratch_shapes=[
            pltpu.SMEM((slots_of, tiles), jnp.int32),
            pltpu.SMEM((1, tiles), jnp.int32),
            pltpu.VMEM(weights.shape, F32),
            pltpu.SemaphoreType.DMA((3,)),
            pltpu.SemaphoreType.DMA,
        ],
    )
    payload, curvature = call(
        functools.partial(gradient_kernel, pair),
        (near((slots + SUB, width)), near((tiles, rows))),
        (labels.reshape(tiles, rows), values_here, ids, *feat_parts(part)),
    )
    halves = pltpu.VMEM((insts * slots, 2 * width), BF16)
    gradient, start_slot, onehot, payload = call(
        functools.partial(start_kernel, insts),
        (
            near((share, width)),
            near((slots, width)),
            near((slots + share, insts * slots), BF16),
            near((tiles + SUB, rows)),
        ),
        (values_here, ids, picked, own, *inst_parts(payload)),
        scratch_shapes=[halves],
    )
    along, payload = call(
        functools.partial(curve_kernel, pair),
        (near((tiles, rows)), near((slots + SUB, width))),
        (values_here, ids, curvature, *feat_parts(payload)),
    )
    next_share, known, payload = call(
        functools.partial(turn_kernel, insts),
        (near((share, width)), near((SUB, width)), near((tiles + SUB, rows))),
        (values_here, onehot, start_slot, gradient, *inst_parts(payload)),
        scratch_shapes=[halves, pltpu.VMEM((slots, width), F32)],
    )
    scalars = call(
        functools.partial(inner_kernel, pair),
        near((SUB, width)),
        (curvature, along, *feat_parts(payload)),
    )
    step = call(
        last_kernel,
        near((share, width)),
        (known, gradient, next_share, *inst_sum_parts(scalars)),
    )
    return (step, gradient)


def solution(mesh):
    in_specs = (
        P("inst", "feat", None, None),
        P("inst", "feat"),
        P("inst", "feat"),
        P("inst"),
        P("feat", None),
    )
    out_specs = (P(("feat", "inst"), None), P(("feat", "inst"), None))
    return jax.shard_map(
        per_device, mesh=mesh, in_specs=in_specs, out_specs=out_specs, check_vma=False
    )
```

```python
import functools

import jax
import jax.numpy as jnp
from jax import lax
from jax.experimental import pallas as pl
from jax.experimental.pallas import tpu as pltpu
from jax.sharding import PartitionSpec as P

F32 = jnp.float32
BF16 = jnp.bfloat16
SUB = 8
LIMIT = 24 * 1024 * 1024


def row_iota(shape):
    return lax.broadcasted_iota(jnp.int32, shape, 0)


def lane_iota(shape):
    return lax.broadcasted_iota(jnp.int32, shape, 1)


def total(array):
    return jnp.sum(jnp.sum(array, axis=0, keepdims=True), axis=1, keepdims=True)


def scalar_rows(width, *scalars):
    lane = lane_iota((SUB, width))
    block = jnp.zeros((SUB, width), F32)
    for place, scalar in enumerate(scalars):
        block = jnp.where(lane == place, scalar, block)
    return block


def read_scalar(block, place):
    lane = lane_iota(block.shape)
    return jnp.sum(jnp.where(lane == place, block, 0.0), axis=1, keepdims=True)


def forward_tile_vector(tile, picked):
    picked = picked.astype(BF16).astype(F32)
    kept = tile[0].astype(F32) * picked[0:1, :]
    for s in range(1, tile.shape[0]):
        kept = kept + tile[s].astype(F32) * picked[s : s + 1, :]
    return jnp.sum(kept.T, axis=0, keepdims=True)


def forward_tile(tile, picked):
    slots, rows, width = tile.shape
    product = lax.dot_general(
        picked.astype(BF16),
        tile.reshape(slots * rows, width),
        (((1,), (1,)), ((), ())),
        preferred_element_type=F32,
    )
    mine = row_iota((slots, rows))
    kept = jnp.where(mine == 0, product[:, :rows], 0.0)
    for s in range(1, slots):
        kept = kept + jnp.where(mine == s, product[:, s * rows : (s + 1) * rows], 0.0)
    return jnp.sum(kept, axis=0, keepdims=True)


def back_tile(tile, rows_term):
    slots, rows, width = tile.shape
    mine = row_iota((slots, rows))
    spread = jnp.concatenate(
        [jnp.where(mine == s, rows_term, 0.0) for s in range(slots)], axis=1
    ).astype(BF16)
    return jnp.dot(spread, tile.reshape(slots * rows, width), preferred_element_type=F32)


def forward_all(values, picked, out):
    tiles, slots = values.shape[:2]
    for t in range(tiles):
        one = forward_tile if t % 4 == 0 else forward_tile_vector
        out[t : t + 1, :] = one(values[t], picked[t * slots : (t + 1) * slots, :])


def back_all(values, rows_term, ids, out):
    tiles, slots = values.shape[:2]
    for t in range(tiles):
        block = slice(t * slots, (t + 1) * slots)
        out[block, :] = jnp.where(
            ids[block, :] >= 0.0, back_tile(values[t], rows_term[t : t + 1, :]), 0.0
        )


def first_kernel(share, columns_in, live_in, weights, values_in, values, ids, picked, own, along,
                 columns, live, weights_here, small_sem, values_sem):
    tiles, slots, rows, width = values.shape
    smalls = [
        pltpu.make_async_copy(columns_in, columns, small_sem.at[0]),
        pltpu.make_async_copy(live_in, live, small_sem.at[1]),
        pltpu.make_async_copy(weights, weights_here, small_sem.at[2]),
    ]
    for small in smalls:
        small.start()
    load = pltpu.make_async_copy(values_in, values, values_sem)
    load.start()
    for small in smalls:
        small.wait()
    for t in range(tiles):
        count = live[0, t]
        for j in range(slots):
            slot = t * slots + j
            column = columns[j, t]
            used = j < count
            row = weights_here[pl.ds(column, 1), :]
            picked[slot : slot + 1, :] = jnp.where(used, row, 0.0)
            ids[slot : slot + 1, :] = jnp.full(
                (1, width), jnp.where(used, column, -2), jnp.int32
            ).astype(F32)
    offset = pl.multiple_of(lax.axis_index("inst") * share, SUB)
    own[...] = weights_here[pl.ds(offset, share), :]
    load.wait()
    forward_all(values, picked, along)


def gradient_kernel(count, labels, values, ids, *refs):
    parts, (payload, curvature) = refs[:count], refs[count:]
    slots = ids.shape[0]
    margin = parts[0][...]
    for part in parts[1:]:
        margin = margin + part[...]
    prob = 1.0 / (1.0 + jnp.exp(-margin))
    curvature[...] = prob * (1.0 - prob)
    back_all(values, prob - labels[...].astype(F32), ids, payload)
    square = ids[...]
    diagonal = row_iota(square.shape) == lane_iota(square.shape)
    sent = jnp.sum(jnp.where(diagonal, square, 0.0), axis=0, keepdims=True)
    sent = jnp.where(sent < 0.0, -1.0, sent)
    payload[slots:, :] = jnp.broadcast_to(sent, (SUB, sent.shape[1]))


def stack_halves(parts, slots, halves):
    width = parts[0].shape[1]
    for k, part in enumerate(parts):
        block = part[:slots, :]
        high = block.astype(BF16)
        halves[k * slots : (k + 1) * slots, :width] = high
        halves[k * slots : (k + 1) * slots, width:] = (block - high.astype(F32)).astype(BF16)


def pick_sums(onehot, halves):
    both = jnp.dot(onehot[...], halves[...], preferred_element_type=F32)
    width = both.shape[1] // 2
    return both[:, :width] + both[:, width:]


def start_kernel(count, values, ids, picked, own, *refs):
    parts = refs[:count]
    gradient, start_slot, onehot, payload, halves = refs[count:]
    tiles = values.shape[0]
    slots, width = ids.shape
    share = own.shape[0]
    offset = lax.axis_index("inst") * share
    blocks = (row_iota((share, width)) + offset).astype(F32)
    for k, part in enumerate(parts):
        sent = part[slots : slots + 1, :]
        place = slice(k * slots, (k + 1) * slots)
        onehot[:slots, place] = jnp.where(ids[...] == sent, 1.0, 0.0).astype(BF16)
        onehot[slots:, place] = jnp.where(blocks == sent, 1.0, 0.0).astype(BF16)
    stack_halves(parts, slots, halves)
    summed = pick_sums(onehot, halves)
    start_slot[...] = -(picked[...] + summed[:slots, :])
    forward_all(values, start_slot, payload)
    slope = own[...] + summed[slots:, :]
    gradient[...] = slope
    payload[tiles:, :] = scalar_rows(width, total(slope * slope))


def curve_kernel(count, values, ids, curvature, *refs):
    parts, (along, payload) = refs[:count], refs[count:]
    tiles = values.shape[0]
    slots, width = ids.shape
    summed = parts[0][...]
    for part in parts[1:]:
        summed = summed + part[...]
    here = summed[:tiles, :]
    along[...] = here
    curved = curvature[...] * here
    back_all(values, curved, ids, payload)
    rounded = curved.astype(BF16).astype(F32)
    norm_part = summed[tiles : tiles + 1, 0:1]
    payload[slots:, :] = scalar_rows(width, norm_part, total(rounded * here))


def turn_kernel(count, values, onehot, start_slot, gradient, *refs):
    parts = refs[:count]
    next_share, known, payload, halves, next_slot = refs[count:]
    tiles = values.shape[0]
    slots, width = start_slot.shape
    scalars = parts[0][slots:, :]
    for part in parts[1:]:
        scalars = scalars + part[slots:, :]
    norm_now = read_scalar(scalars[0:1, :], 0)
    curve_now = read_scalar(scalars[0:1, :], 1)
    alpha = norm_now / (norm_now + curve_now)
    stack_halves(parts, slots, halves)
    summed = pick_sums(onehot, halves)
    start = start_slot[...]
    next_slot[...] = start - alpha * (start + summed[:slots, :])
    forward_all(values, next_slot, payload)
    start_own = -gradient[...]
    turned = start_own - alpha * (start_own + summed[slots:, :])
    next_share[...] = turned
    payload[tiles:, :] = scalar_rows(width, total(turned * turned), total(turned * start_own))
    known[...] = scalar_rows(width, norm_now, curve_now, alpha)


def inner_kernel(count, curvature, along, *refs):
    parts, (scalars,) = refs[:count], refs[count:]
    tiles, width = along.shape
    summed = parts[0][...]
    for part in parts[1:]:
        summed = summed + part[...]
    turn = summed[:tiles, :]
    bent = curvature[...] * turn
    scalars[...] = scalar_rows(
        width,
        summed[tiles : tiles + 1, 0:1],
        summed[tiles : tiles + 1, 1:2],
        total(bent * turn),
        total(bent * along[...]),
    )


def last_kernel(known, gradient, next_share, *refs):
    parts, step = refs[:-1], refs[-1]
    row = parts[0][0:1, :]
    for part in parts[1:]:
        row = row + part[0:1, :]
    norm_next, cross, turn_turn, turn_along = (read_scalar(row, i) for i in range(4))
    row = known[0:1, :]
    norm_now, curve_now, alpha = (read_scalar(row, i) for i in range(3))
    ratio = norm_next / norm_now
    bottom = (
        norm_next
        + turn_turn
        + 2.0 * ratio * (cross + turn_along)
        + ratio * ratio * (norm_now + curve_now)
    )
    alpha_next = norm_next / bottom
    start = -gradient[...]
    step[...] = alpha * start + alpha_next * (next_share[...] + ratio * start)


def near(shape, dtype=F32):
    return pltpu.VMEM(shape, dtype)


def call(kernel, out_shape, args, in_specs=None, scratch_shapes=()):
    vmem = pl.BlockSpec(memory_space=pltpu.VMEM)
    if in_specs is None:
        in_specs = [vmem] * len(args)
        args = [pltpu.with_memory_space_constraint(a, pltpu.VMEM) for a in args]
    return pl.pallas_call(
        kernel,
        out_shape=out_shape,
        in_specs=in_specs,
        out_specs=jax.tree.map(lambda _: vmem, out_shape),
        scratch_shapes=list(scratch_shapes),
        compiler_params=pltpu.CompilerParams(vmem_limit_bytes=LIMIT),
    )(*args)


def swap(array, axis, distance):
    size = lax.axis_size(axis)
    return lax.ppermute(array, axis, [(i, i ^ distance) for i in range(size)])


def swap_both(array, distance):
    size, feats = lax.axis_size("inst"), lax.axis_size("feat")
    pairs = [
        (i * feats + f, (i ^ distance) * feats + (f ^ 1))
        for i in range(size)
        for f in range(feats)
    ]
    return lax.ppermute(array, ("inst", "feat"), pairs)


def feat_parts(array):
    distance = 1
    parts = [array]
    while distance < lax.axis_size("feat"):
        array = sum(parts[1:], parts[0])
        parts = [array, swap(array, "feat", distance | 1)]
        distance *= 2
    return parts


def inst_parts(array):
    size = lax.axis_size("inst")
    if size != 8:
        gathered = lax.all_gather(array, "inst", axis=0)
        return [gathered[i] for i in range(size)]
    parts = {0: array}
    for distance in (2, 4, 6, 1, 3):
        parts[distance] = swap(array, "inst", distance)
    for distance in (4, 6):
        parts[distance ^ 1] = swap(parts[distance], "inst", 1)
    return list(parts.values())


def inst_sum_parts(array):
    size = lax.axis_size("inst")
    stages = [(2, 4, 6), (1,)] if size == 8 else [(1 << b,) for b in range(size.bit_length() - 1)]
    parts = [array]
    for stage in stages:
        array = sum(parts[1:], parts[0])
        parts = [array] + [swap_both(array, distance) for distance in stage]
    return parts


def per_device(values, columns, live_slots, labels, weights):
    tiles, slots_of, rows, width = values.shape
    slots = tiles * slots_of
    share = weights.shape[0] // lax.axis_size("inst")
    insts, pair = lax.axis_size("inst"), 2

    values_here, ids, picked, own, part = call(
        functools.partial(first_kernel, share),
        (
            near(values.shape, BF16),
            near((slots, width)),
            near((slots, width)),
            near((share, width)),
            near((tiles, rows)),
        ),
        [
            pltpu.with_memory_space_constraint(a, pltpu.HBM)
            for a in (columns.T, live_slots.T, weights, values)
        ],
        in_specs=[pl.BlockSpec(memory_space=pltpu.HBM)] * 4,
        scratch_shapes=[
            pltpu.SMEM((slots_of, tiles), jnp.int32),
            pltpu.SMEM((1, tiles), jnp.int32),
            pltpu.VMEM(weights.shape, F32),
            pltpu.SemaphoreType.DMA((3,)),
            pltpu.SemaphoreType.DMA,
        ],
    )
    payload, curvature = call(
        functools.partial(gradient_kernel, pair),
        (near((slots + SUB, width)), near((tiles, rows))),
        (labels.reshape(tiles, rows), values_here, ids, *feat_parts(part)),
    )
    halves = pltpu.VMEM((insts * slots, 2 * width), BF16)
    gradient, start_slot, onehot, payload = call(
        functools.partial(start_kernel, insts),
        (
            near((share, width)),
            near((slots, width)),
            near((slots + share, insts * slots), BF16),
            near((tiles + SUB, rows)),
        ),
        (values_here, ids, picked, own, *inst_parts(payload)),
        scratch_shapes=[halves],
    )
    along, payload = call(
        functools.partial(curve_kernel, pair),
        (near((tiles, rows)), near((slots + SUB, width))),
        (values_here, ids, curvature, *feat_parts(payload)),
    )
    next_share, known, payload = call(
        functools.partial(turn_kernel, insts),
        (near((share, width)), near((SUB, width)), near((tiles + SUB, rows))),
        (values_here, onehot, start_slot, gradient, *inst_parts(payload)),
        scratch_shapes=[halves, pltpu.VMEM((slots, width), F32)],
    )
    scalars = call(
        functools.partial(inner_kernel, pair),
        near((SUB, width)),
        (curvature, along, *feat_parts(payload)),
    )
    step = call(
        last_kernel,
        near((share, width)),
        (known, gradient, next_share, *inst_sum_parts(scalars)),
    )
    return (step, gradient)


def solution(mesh):
    in_specs = (
        P("inst", "feat", None, None),
        P("inst", "feat"),
        P("inst", "feat"),
        P("inst"),
        P("feat", None),
    )
    out_specs = (P(("feat", "inst"), None), P(("feat", "inst"), None))
    return jax.shard_map(
        per_device, mesh=mesh, in_specs=in_specs, out_specs=out_specs, check_vma=False
    )
```

```python
import functools

import jax
import jax.numpy as jnp
from jax import lax
from jax.experimental import pallas as pl
from jax.experimental.pallas import tpu as pltpu
from jax.sharding import PartitionSpec as P

F32 = jnp.float32
BF16 = jnp.bfloat16
SUB = 8
LIMIT = 24 * 1024 * 1024


def row_iota(shape):
    return lax.broadcasted_iota(jnp.int32, shape, 0)


def lane_iota(shape):
    return lax.broadcasted_iota(jnp.int32, shape, 1)


def total(array):
    return jnp.sum(jnp.sum(array, axis=0, keepdims=True), axis=1, keepdims=True)


def scalar_rows(width, *scalars):
    lane = lane_iota((SUB, width))
    block = jnp.zeros((SUB, width), F32)
    for place, scalar in enumerate(scalars):
        block = jnp.where(lane == place, scalar, block)
    return block


def read_scalar(block, place):
    lane = lane_iota(block.shape)
    return jnp.sum(jnp.where(lane == place, block, 0.0), axis=1, keepdims=True)


def forward_tile_vector(tile, picked):
    picked = picked.astype(BF16).astype(F32)
    kept = tile[0].astype(F32) * picked[0:1, :]
    for s in range(1, tile.shape[0]):
        kept = kept + tile[s].astype(F32) * picked[s : s + 1, :]
    return jnp.sum(kept.T, axis=0, keepdims=True)


def forward_tile(tile, picked):
    slots, rows, width = tile.shape
    product = lax.dot_general(
        picked.astype(BF16),
        tile.reshape(slots * rows, width),
        (((1,), (1,)), ((), ())),
        preferred_element_type=F32,
    )
    mine = row_iota((slots, rows))
    kept = jnp.where(mine == 0, product[:, :rows], 0.0)
    for s in range(1, slots):
        kept = kept + jnp.where(mine == s, product[:, s * rows : (s + 1) * rows], 0.0)
    return jnp.sum(kept, axis=0, keepdims=True)


def back_tile(tile, rows_term):
    slots, rows, width = tile.shape
    mine = row_iota((slots, rows))
    spread = jnp.concatenate(
        [jnp.where(mine == s, rows_term, 0.0) for s in range(slots)], axis=1
    ).astype(BF16)
    return jnp.dot(spread, tile.reshape(slots * rows, width), preferred_element_type=F32)


def forward_all(values, picked, out):
    tiles, slots = values.shape[:2]
    for t in range(tiles):
        one = forward_tile if t % 4 == 0 else forward_tile_vector
        out[t : t + 1, :] = one(values[t], picked[t * slots : (t + 1) * slots, :])


def back_all(values, rows_term, ids, out):
    tiles, slots = values.shape[:2]
    for t in range(tiles):
        block = slice(t * slots, (t + 1) * slots)
        out[block, :] = jnp.where(
            ids[block, :] >= 0.0, back_tile(values[t], rows_term[t : t + 1, :]), 0.0
        )


def first_kernel(share, columns_in, live_in, weights, values_in, values, ids, picked, own, along,
                 columns, live, weights_here, small_sem, values_sem):
    tiles, slots, rows, width = values.shape
    smalls = [
        pltpu.make_async_copy(columns_in, columns, small_sem.at[0]),
        pltpu.make_async_copy(live_in, live, small_sem.at[1]),
        pltpu.make_async_copy(weights, weights_here, small_sem.at[2]),
    ]
    for small in smalls:
        small.start()
    load = pltpu.make_async_copy(values_in, values, values_sem)
    load.start()
    for small in smalls:
        small.wait()
    for t in range(tiles):
        count = live[0, t]
        for j in range(slots):
            slot = t * slots + j
            column = columns[j, t]
            used = j < count
            row = weights_here[pl.ds(column, 1), :]
            picked[slot : slot + 1, :] = jnp.where(used, row, 0.0)
            ids[slot : slot + 1, :] = jnp.full(
                (1, width), jnp.where(used, column, -2), jnp.int32
            ).astype(F32)
    offset = pl.multiple_of(lax.axis_index("inst") * share, SUB)
    own[...] = weights_here[pl.ds(offset, share), :]
    load.wait()
    forward_all(values, picked, along)


def gradient_kernel(count, labels, values, ids, *refs):
    parts, (payload, curvature) = refs[:count], refs[count:]
    slots = ids.shape[0]
    margin = parts[0][...]
    for part in parts[1:]:
        margin = margin + part[...]
    prob = 1.0 / (1.0 + jnp.exp(-margin))
    curvature[...] = prob * (1.0 - prob)
    back_all(values, prob - labels[...].astype(F32), ids, payload)
    square = ids[...]
    diagonal = row_iota(square.shape) == lane_iota(square.shape)
    sent = jnp.sum(jnp.where(diagonal, square, 0.0), axis=0, keepdims=True)
    sent = jnp.where(sent < 0.0, -1.0, sent)
    payload[slots:, :] = jnp.broadcast_to(sent, (SUB, sent.shape[1]))


def stack_halves(parts, slots, halves):
    width = parts[0].shape[1]
    for k, part in enumerate(parts):
        block = part[:slots, :]
        high = block.astype(BF16)
        halves[k * slots : (k + 1) * slots, :width] = high
        halves[k * slots : (k + 1) * slots, width:] = (block - high.astype(F32)).astype(BF16)


def pick_sums(onehot, halves):
    both = jnp.dot(onehot, halves[...], preferred_element_type=F32)
    width = both.shape[1] // 2
    return both[:, :width] + both[:, width:]


def start_kernel(count, values, ids, picked, own, *refs):
    parts = refs[:count]
    gradient, start_slot, onehot, payload, halves = refs[count:]
    tiles = values.shape[0]
    slots, width = ids.shape
    share = own.shape[0]
    offset = lax.axis_index("inst") * share
    blocks = (row_iota((share, width)) + offset).astype(F32)
    for k, part in enumerate(parts):
        sent = part[slots : slots + 1, :]
        place = slice(k * slots, (k + 1) * slots)
        onehot[:slots, place] = jnp.where(ids[...] == sent, 1.0, 0.0).astype(BF16)
        onehot[slots:, place] = jnp.where(blocks == sent, 1.0, 0.0).astype(BF16)
    stack_halves(parts, slots, halves)
    start_slot[...] = -(picked[...] + pick_sums(onehot[:slots, :], halves))
    slope = own[...] + pick_sums(onehot[slots:, :], halves)
    gradient[...] = slope
    forward_all(values, start_slot, payload)
    payload[tiles:, :] = scalar_rows(width, total(slope * slope))


def curve_kernel(count, values, ids, curvature, *refs):
    parts, (along, payload) = refs[:count], refs[count:]
    tiles = values.shape[0]
    slots, width = ids.shape
    summed = parts[0][...]
    for part in parts[1:]:
        summed = summed + part[...]
    here = summed[:tiles, :]
    along[...] = here
    curved = curvature[...] * here
    back_all(values, curved, ids, payload)
    rounded = curved.astype(BF16).astype(F32)
    norm_part = summed[tiles : tiles + 1, 0:1]
    payload[slots:, :] = scalar_rows(width, norm_part, total(rounded * here))


def turn_kernel(count, values, onehot, start_slot, gradient, *refs):
    parts = refs[:count]
    next_share, known, payload, halves, next_slot = refs[count:]
    tiles = values.shape[0]
    slots, width = start_slot.shape
    scalars = parts[0][slots:, :]
    for part in parts[1:]:
        scalars = scalars + part[slots:, :]
    norm_now = read_scalar(scalars[0:1, :], 0)
    curve_now = read_scalar(scalars[0:1, :], 1)
    alpha = norm_now / (norm_now + curve_now)
    stack_halves(parts, slots, halves)
    start = start_slot[...]
    next_slot[...] = start - alpha * (start + pick_sums(onehot[:slots, :], halves))
    start_own = -gradient[...]
    turned = start_own - alpha * (start_own + pick_sums(onehot[slots:, :], halves))
    next_share[...] = turned
    forward_all(values, next_slot, payload)
    payload[tiles:, :] = scalar_rows(width, total(turned * turned), total(turned * start_own))
    known[...] = scalar_rows(width, norm_now, curve_now, alpha)


def inner_kernel(count, curvature, along, *refs):
    parts, (scalars,) = refs[:count], refs[count:]
    tiles, width = along.shape
    summed = parts[0][...]
    for part in parts[1:]:
        summed = summed + part[...]
    turn = summed[:tiles, :]
    bent = curvature[...] * turn
    scalars[...] = scalar_rows(
        width,
        summed[tiles : tiles + 1, 0:1],
        summed[tiles : tiles + 1, 1:2],
        total(bent * turn),
        total(bent * along[...]),
    )


def last_kernel(known, gradient, next_share, *refs):
    parts, step = refs[:-1], refs[-1]
    row = parts[0][0:1, :]
    for part in parts[1:]:
        row = row + part[0:1, :]
    norm_next, cross, turn_turn, turn_along = (read_scalar(row, i) for i in range(4))
    row = known[0:1, :]
    norm_now, curve_now, alpha = (read_scalar(row, i) for i in range(3))
    ratio = norm_next / norm_now
    bottom = (
        norm_next
        + turn_turn
        + 2.0 * ratio * (cross + turn_along)
        + ratio * ratio * (norm_now + curve_now)
    )
    alpha_next = norm_next / bottom
    start = -gradient[...]
    step[...] = alpha * start + alpha_next * (next_share[...] + ratio * start)


def near(shape, dtype=F32):
    return pltpu.VMEM(shape, dtype)


def call(kernel, out_shape, args, in_specs=None, scratch_shapes=()):
    vmem = pl.BlockSpec(memory_space=pltpu.VMEM)
    if in_specs is None:
        in_specs = [vmem] * len(args)
        args = [pltpu.with_memory_space_constraint(a, pltpu.VMEM) for a in args]
    return pl.pallas_call(
        kernel,
        out_shape=out_shape,
        in_specs=in_specs,
        out_specs=jax.tree.map(lambda _: vmem, out_shape),
        scratch_shapes=list(scratch_shapes),
        compiler_params=pltpu.CompilerParams(vmem_limit_bytes=LIMIT),
    )(*args)


def swap(array, axis, distance):
    size = lax.axis_size(axis)
    return lax.ppermute(array, axis, [(i, i ^ distance) for i in range(size)])


def swap_both(array, distance):
    size, feats = lax.axis_size("inst"), lax.axis_size("feat")
    pairs = [
        (i * feats + f, (i ^ distance) * feats + (f ^ 1))
        for i in range(size)
        for f in range(feats)
    ]
    return lax.ppermute(array, ("inst", "feat"), pairs)


def feat_parts(array):
    distance = 1
    parts = [array]
    while distance < lax.axis_size("feat"):
        array = sum(parts[1:], parts[0])
        parts = [array, swap(array, "feat", distance | 1)]
        distance *= 2
    return parts


def inst_parts(array):
    size = lax.axis_size("inst")
    if size != 8:
        gathered = lax.all_gather(array, "inst", axis=0)
        return [gathered[i] for i in range(size)]
    parts = {0: array}
    for distance in (2, 6, 3, 1, 4):
        parts[distance] = swap(array, "inst", distance)
    for distance in (4, 6):
        parts[distance ^ 1] = swap(parts[distance], "inst", 1)
    return list(parts.values())


def inst_sum_parts(array):
    size = lax.axis_size("inst")
    stages = [(2, 4, 6), (1,)] if size == 8 else [(1 << b,) for b in range(size.bit_length() - 1)]
    parts = [array]
    for stage in stages:
        array = sum(parts[1:], parts[0])
        parts = [array] + [swap_both(array, distance) for distance in stage]
    return parts


def per_device(values, columns, live_slots, labels, weights):
    tiles, slots_of, rows, width = values.shape
    slots = tiles * slots_of
    share = weights.shape[0] // lax.axis_size("inst")
    insts, pair = lax.axis_size("inst"), 2

    values_here, ids, picked, own, part = call(
        functools.partial(first_kernel, share),
        (
            near(values.shape, BF16),
            near((slots, width)),
            near((slots, width)),
            near((share, width)),
            near((tiles, rows)),
        ),
        [
            pltpu.with_memory_space_constraint(a, pltpu.HBM)
            for a in (columns.T, live_slots.T, weights, values)
        ],
        in_specs=[pl.BlockSpec(memory_space=pltpu.HBM)] * 4,
        scratch_shapes=[
            pltpu.SMEM((slots_of, tiles), jnp.int32),
            pltpu.SMEM((1, tiles), jnp.int32),
            pltpu.VMEM(weights.shape, F32),
            pltpu.SemaphoreType.DMA((3,)),
            pltpu.SemaphoreType.DMA,
        ],
    )
    payload, curvature = call(
        functools.partial(gradient_kernel, pair),
        (near((slots + SUB, width)), near((tiles, rows))),
        (labels.reshape(tiles, rows), values_here, ids, *feat_parts(part)),
    )
    halves = pltpu.VMEM((insts * slots, 2 * width), BF16)
    gradient, start_slot, onehot, payload = call(
        functools.partial(start_kernel, insts),
        (
            near((share, width)),
            near((slots, width)),
            near((slots + share, insts * slots), BF16),
            near((tiles + SUB, rows)),
        ),
        (values_here, ids, picked, own, *inst_parts(payload)),
        scratch_shapes=[halves],
    )
    along, payload = call(
        functools.partial(curve_kernel, pair),
        (near((tiles, rows)), near((slots + SUB, width))),
        (values_here, ids, curvature, *feat_parts(payload)),
    )
    next_share, known, payload = call(
        functools.partial(turn_kernel, insts),
        (near((share, width)), near((SUB, width)), near((tiles + SUB, rows))),
        (values_here, onehot, start_slot, gradient, *inst_parts(payload)),
        scratch_shapes=[halves, pltpu.VMEM((slots, width), F32)],
    )
    scalars = call(
        functools.partial(inner_kernel, pair),
        near((SUB, width)),
        (curvature, along, *feat_parts(payload)),
    )
    step = call(
        last_kernel,
        near((share, width)),
        (known, gradient, next_share, *inst_sum_parts(scalars)),
    )
    return (step, gradient)


def solution(mesh):
    in_specs = (
        P("inst", "feat", None, None),
        P("inst", "feat"),
        P("inst", "feat"),
        P("inst"),
        P("feat", None),
    )
    out_specs = (P(("feat", "inst"), None), P(("feat", "inst"), None))
    return jax.shard_map(
        per_device, mesh=mesh, in_specs=in_specs, out_specs=out_specs, check_vma=False
    )
```

```python
import functools

import jax
import jax.numpy as jnp
from jax import lax
from jax.experimental import pallas as pl
from jax.experimental.pallas import tpu as pltpu
from jax.sharding import PartitionSpec as P

F32 = jnp.float32
BF16 = jnp.bfloat16
SUB = 8
LIMIT = 24 * 1024 * 1024


def row_iota(shape):
    return lax.broadcasted_iota(jnp.int32, shape, 0)


def lane_iota(shape):
    return lax.broadcasted_iota(jnp.int32, shape, 1)


def total(array):
    return jnp.sum(jnp.sum(array, axis=0, keepdims=True), axis=1, keepdims=True)


def scalar_rows(width, *scalars):
    lane = lane_iota((SUB, width))
    block = jnp.zeros((SUB, width), F32)
    for place, scalar in enumerate(scalars):
        block = jnp.where(lane == place, scalar, block)
    return block


def read_scalar(block, place):
    lane = lane_iota(block.shape)
    return jnp.sum(jnp.where(lane == place, block, 0.0), axis=1, keepdims=True)


def forward_tile_vector(tile, picked):
    picked = picked.astype(BF16).astype(F32)
    kept = tile[0].astype(F32) * picked[0:1, :]
    for s in range(1, tile.shape[0]):
        kept = kept + tile[s].astype(F32) * picked[s : s + 1, :]
    return jnp.sum(kept.T, axis=0, keepdims=True)


def forward_tile(tile, picked):
    slots, rows, width = tile.shape
    product = lax.dot_general(
        picked.astype(BF16),
        tile.reshape(slots * rows, width),
        (((1,), (1,)), ((), ())),
        preferred_element_type=F32,
    )
    mine = row_iota((slots, rows))
    kept = jnp.where(mine == 0, product[:, :rows], 0.0)
    for s in range(1, slots):
        kept = kept + jnp.where(mine == s, product[:, s * rows : (s + 1) * rows], 0.0)
    return jnp.sum(kept, axis=0, keepdims=True)


def back_tile(tile, rows_term):
    slots, rows, width = tile.shape
    mine = row_iota((slots, rows))
    spread = jnp.concatenate(
        [jnp.where(mine == s, rows_term, 0.0) for s in range(slots)], axis=1
    ).astype(BF16)
    return jnp.dot(spread, tile.reshape(slots * rows, width), preferred_element_type=F32)


def forward_all(values, picked, out):
    tiles, slots = values.shape[:2]
    for t in range(tiles):
        one = forward_tile if t % 4 == 0 else forward_tile_vector
        out[t : t + 1, :] = one(values[t], picked[t * slots : (t + 1) * slots, :])


def back_all(values, rows_term, ids, out):
    tiles, slots = values.shape[:2]
    for t in range(tiles):
        block = slice(t * slots, (t + 1) * slots)
        out[block, :] = jnp.where(
            ids[block, :] >= 0.0, back_tile(values[t], rows_term[t : t + 1, :]), 0.0
        )


def first_kernel(share, columns_in, live_in, weights, values_in, values, ids, picked, own, along,
                 columns, live, weights_here, small_sem, values_sem):
    tiles, slots, rows, width = values.shape
    smalls = [
        pltpu.make_async_copy(columns_in, columns, small_sem.at[0]),
        pltpu.make_async_copy(live_in, live, small_sem.at[1]),
        pltpu.make_async_copy(weights, weights_here, small_sem.at[2]),
    ]
    for small in smalls:
        small.start()
    load = pltpu.make_async_copy(values_in, values, values_sem)
    load.start()
    for small in smalls:
        small.wait()
    for t in range(tiles):
        count = live[0, t]
        for j in range(slots):
            slot = t * slots + j
            column = columns[j, t]
            used = j < count
            row = weights_here[pl.ds(column, 1), :]
            picked[slot : slot + 1, :] = jnp.where(used, row, 0.0)
            ids[slot : slot + 1, :] = jnp.full(
                (1, width), jnp.where(used, column, -2), jnp.int32
            ).astype(F32)
    offset = pl.multiple_of(lax.axis_index("inst") * share, SUB)
    own[...] = weights_here[pl.ds(offset, share), :]
    load.wait()
    forward_all(values, picked, along)


def gradient_kernel(count, labels, values, ids, *refs):
    parts, (payload, curvature) = refs[:count], refs[count:]
    slots = ids.shape[0]
    margin = parts[0][...]
    for part in parts[1:]:
        margin = margin + part[...]
    prob = 1.0 / (1.0 + jnp.exp(-margin))
    curvature[...] = prob * (1.0 - prob)
    back_all(values, prob - labels[...].astype(F32), ids, payload)
    square = ids[...]
    diagonal = row_iota(square.shape) == lane_iota(square.shape)
    sent = jnp.sum(jnp.where(diagonal, square, 0.0), axis=0, keepdims=True)
    sent = jnp.where(sent < 0.0, -1.0, sent)
    payload[slots:, :] = jnp.broadcast_to(sent, (SUB, sent.shape[1]))


def stack_halves(parts, slots, halves):
    width = parts[0].shape[1]
    for k, part in enumerate(parts):
        block = part[:slots, :]
        high = block.astype(BF16)
        halves[k * slots : (k + 1) * slots, :width] = high
        halves[k * slots : (k + 1) * slots, width:] = (block - high.astype(F32)).astype(BF16)


def pick_sums(onehot, halves):
    both = jnp.dot(onehot, halves[...], preferred_element_type=F32)
    width = both.shape[1] // 2
    return both[:, :width] + both[:, width:]


def start_kernel(count, values, ids, picked, own, *refs):
    parts = refs[:count]
    gradient, start_slot, onehot, payload, halves = refs[count:]
    tiles = values.shape[0]
    slots, width = ids.shape
    share = own.shape[0]
    offset = lax.axis_index("inst") * share
    blocks = (row_iota((share, width)) + offset).astype(F32)
    for k, part in enumerate(parts):
        sent = part[slots : slots + 1, :]
        place = slice(k * slots, (k + 1) * slots)
        onehot[:slots, place] = jnp.where(ids[...] == sent, 1.0, 0.0).astype(BF16)
        onehot[slots:, place] = jnp.where(blocks == sent, 1.0, 0.0).astype(BF16)
    stack_halves(parts, slots, halves)
    start_slot[...] = -(picked[...] + pick_sums(onehot[:slots, :], halves))
    slope = own[...] + pick_sums(onehot[slots:, :], halves)
    gradient[...] = slope
    forward_all(values, start_slot, payload)
    payload[tiles:, :] = scalar_rows(width, total(slope * slope))


def curve_kernel(count, values, ids, curvature, *refs):
    parts, (along, payload) = refs[:count], refs[count:]
    tiles = values.shape[0]
    slots, width = ids.shape
    summed = parts[0][...]
    for part in parts[1:]:
        summed = summed + part[...]
    here = summed[:tiles, :]
    along[...] = here
    curved = curvature[...] * here
    back_all(values, curved, ids, payload)
    rounded = curved.astype(BF16).astype(F32)
    norm_part = summed[tiles : tiles + 1, 0:1]
    payload[slots:, :] = scalar_rows(width, norm_part, total(rounded * here))


def turn_kernel(count, values, onehot, start_slot, gradient, *refs):
    parts = refs[:count]
    next_share, known, payload, halves, next_slot = refs[count:]
    tiles = values.shape[0]
    slots, width = start_slot.shape
    scalars = parts[0][slots:, :]
    for part in parts[1:]:
        scalars = scalars + part[slots:, :]
    norm_now = read_scalar(scalars[0:1, :], 0)
    curve_now = read_scalar(scalars[0:1, :], 1)
    alpha = norm_now / (norm_now + curve_now)
    stack_halves(parts, slots, halves)
    start = start_slot[...]
    next_slot[...] = start - alpha * (start + pick_sums(onehot[:slots, :], halves))
    start_own = -gradient[...]
    turned = start_own - alpha * (start_own + pick_sums(onehot[slots:, :], halves))
    next_share[...] = turned
    forward_all(values, next_slot, payload)
    payload[tiles:, :] = scalar_rows(width, total(turned * turned), total(turned * start_own))
    known[...] = scalar_rows(width, norm_now, curve_now, alpha)


def inner_kernel(count, curvature, along, *refs):
    parts, (scalars,) = refs[:count], refs[count:]
    tiles, width = along.shape
    summed = parts[0][...]
    for part in parts[1:]:
        summed = summed + part[...]
    turn = summed[:tiles, :]
    bent = curvature[...] * turn
    scalars[...] = scalar_rows(
        width,
        summed[tiles : tiles + 1, 0:1],
        summed[tiles : tiles + 1, 1:2],
        total(bent * turn),
        total(bent * along[...]),
    )


def last_kernel(known, gradient, next_share, *refs):
    parts, step = refs[:-1], refs[-1]
    row = parts[0][0:1, :]
    for part in parts[1:]:
        row = row + part[0:1, :]
    norm_next, cross, turn_turn, turn_along = (read_scalar(row, i) for i in range(4))
    row = known[0:1, :]
    norm_now, curve_now, alpha = (read_scalar(row, i) for i in range(3))
    ratio = norm_next / norm_now
    bottom = (
        norm_next
        + turn_turn
        + 2.0 * ratio * (cross + turn_along)
        + ratio * ratio * (norm_now + curve_now)
    )
    alpha_next = norm_next / bottom
    start = -gradient[...]
    step[...] = alpha * start + alpha_next * (next_share[...] + ratio * start)


def near(shape, dtype=F32):
    return pltpu.VMEM(shape, dtype)


def call(kernel, out_shape, args, in_specs=None, scratch_shapes=()):
    vmem = pl.BlockSpec(memory_space=pltpu.VMEM)
    if in_specs is None:
        in_specs = [vmem] * len(args)
        args = [pltpu.with_memory_space_constraint(a, pltpu.VMEM) for a in args]
    return pl.pallas_call(
        kernel,
        out_shape=out_shape,
        in_specs=in_specs,
        out_specs=jax.tree.map(lambda _: vmem, out_shape),
        scratch_shapes=list(scratch_shapes),
        compiler_params=pltpu.CompilerParams(vmem_limit_bytes=LIMIT),
    )(*args)


def swap(array, axis, distance):
    size = lax.axis_size(axis)
    return lax.ppermute(array, axis, [(i, i ^ distance) for i in range(size)])


def swap_both(array, distance):
    size, feats = lax.axis_size("inst"), lax.axis_size("feat")
    pairs = [
        (i * feats + f, (i ^ distance) * feats + (f ^ 1))
        for i in range(size)
        for f in range(feats)
    ]
    return lax.ppermute(array, ("inst", "feat"), pairs)


def feat_parts(array):
    distance = 1
    parts = [array]
    while distance < lax.axis_size("feat"):
        array = sum(parts[1:], parts[0])
        parts = [array, swap(array, "feat", distance | 1)]
        distance *= 2
    return parts


def inst_parts(array):
    size = lax.axis_size("inst")
    if size != 8:
        gathered = lax.all_gather(array, "inst", axis=0)
        return [gathered[i] for i in range(size)]
    parts = {0: array}
    for distance in (2, 4, 6, 1, 3):
        parts[distance] = swap(array, "inst", distance)
    for distance in (4, 6):
        parts[distance ^ 1] = swap(parts[distance], "inst", 1)
    return list(parts.values())


def inst_sum_parts(array):
    size = lax.axis_size("inst")
    stages = [(1, 2, 3), (4,)] if size == 8 else [(1 << b,) for b in range(size.bit_length() - 1)]
    parts = [array]
    for stage in stages:
        array = sum(parts[1:], parts[0])
        parts = [array] + [swap_both(array, distance) for distance in stage]
    return parts


def per_device(values, columns, live_slots, labels, weights):
    tiles, slots_of, rows, width = values.shape
    slots = tiles * slots_of
    share = weights.shape[0] // lax.axis_size("inst")
    insts, pair = lax.axis_size("inst"), 2

    values_here, ids, picked, own, part = call(
        functools.partial(first_kernel, share),
        (
            near(values.shape, BF16),
            near((slots, width)),
            near((slots, width)),
            near((share, width)),
            near((tiles, rows)),
        ),
        [
            pltpu.with_memory_space_constraint(a, pltpu.HBM)
            for a in (columns.T, live_slots.T, weights, values)
        ],
        in_specs=[pl.BlockSpec(memory_space=pltpu.HBM)] * 4,
        scratch_shapes=[
            pltpu.SMEM((slots_of, tiles), jnp.int32),
            pltpu.SMEM((1, tiles), jnp.int32),
            pltpu.VMEM(weights.shape, F32),
            pltpu.SemaphoreType.DMA((3,)),
            pltpu.SemaphoreType.DMA,
        ],
    )
    payload, curvature = call(
        functools.partial(gradient_kernel, pair),
        (near((slots + SUB, width)), near((tiles, rows))),
        (labels.reshape(tiles, rows), values_here, ids, *feat_parts(part)),
    )
    halves = pltpu.VMEM((insts * slots, 2 * width), BF16)
    gradient, start_slot, onehot, payload = call(
        functools.partial(start_kernel, insts),
        (
            near((share, width)),
            near((slots, width)),
            near((slots + share, insts * slots), BF16),
            near((tiles + SUB, rows)),
        ),
        (values_here, ids, picked, own, *inst_parts(payload)),
        scratch_shapes=[halves],
    )
    along, payload = call(
        functools.partial(curve_kernel, pair),
        (near((tiles, rows)), near((slots + SUB, width))),
        (values_here, ids, curvature, *feat_parts(payload)),
    )
    next_share, known, payload = call(
        functools.partial(turn_kernel, insts),
        (near((share, width)), near((SUB, width)), near((tiles + SUB, rows))),
        (values_here, onehot, start_slot, gradient, *inst_parts(payload)),
        scratch_shapes=[halves, pltpu.VMEM((slots, width), F32)],
    )
    scalars = call(
        functools.partial(inner_kernel, pair),
        near((SUB, width)),
        (curvature, along, *feat_parts(payload)),
    )
    step = call(
        last_kernel,
        near((share, width)),
        (known, gradient, next_share, *inst_sum_parts(scalars)),
    )
    return (step, gradient)


def solution(mesh):
    in_specs = (
        P("inst", "feat", None, None),
        P("inst", "feat"),
        P("inst", "feat"),
        P("inst"),
        P("feat", None),
    )
    out_specs = (P(("feat", "inst"), None), P(("feat", "inst"), None))
    return jax.shard_map(
        per_device, mesh=mesh, in_specs=in_specs, out_specs=out_specs, check_vma=False
    )
```

```python
import functools

import jax
import jax.numpy as jnp
from jax import lax
from jax.experimental import pallas as pl
from jax.experimental.pallas import tpu as pltpu
from jax.sharding import PartitionSpec as P

F32 = jnp.float32
BF16 = jnp.bfloat16
SUB = 8
LIMIT = 24 * 1024 * 1024


def row_iota(shape):
    return lax.broadcasted_iota(jnp.int32, shape, 0)


def lane_iota(shape):
    return lax.broadcasted_iota(jnp.int32, shape, 1)


def total(array):
    return jnp.sum(jnp.sum(array, axis=0, keepdims=True), axis=1, keepdims=True)


def scalar_rows(width, *scalars):
    lane = lane_iota((SUB, width))
    block = jnp.zeros((SUB, width), F32)
    for place, scalar in enumerate(scalars):
        block = jnp.where(lane == place, scalar, block)
    return block


def read_scalar(block, place):
    lane = lane_iota(block.shape)
    return jnp.sum(jnp.where(lane == place, block, 0.0), axis=1, keepdims=True)


def forward_tile_vector(tile, picked):
    picked = picked.astype(BF16).astype(F32)
    kept = tile[0].astype(F32) * picked[0:1, :]
    for s in range(1, tile.shape[0]):
        kept = kept + tile[s].astype(F32) * picked[s : s + 1, :]
    return jnp.sum(kept.T, axis=0, keepdims=True)


def forward_tile(tile, picked):
    slots, rows, width = tile.shape
    product = lax.dot_general(
        picked.astype(BF16),
        tile.reshape(slots * rows, width),
        (((1,), (1,)), ((), ())),
        preferred_element_type=F32,
    )
    mine = row_iota((slots, rows))
    kept = jnp.where(mine == 0, product[:, :rows], 0.0)
    for s in range(1, slots):
        kept = kept + jnp.where(mine == s, product[:, s * rows : (s + 1) * rows], 0.0)
    return jnp.sum(kept, axis=0, keepdims=True)


def back_tile(tile, rows_term):
    slots, rows, width = tile.shape
    mine = row_iota((slots, rows))
    spread = jnp.concatenate(
        [jnp.where(mine == s, rows_term, 0.0) for s in range(slots)], axis=1
    ).astype(BF16)
    return jnp.dot(spread, tile.reshape(slots * rows, width), preferred_element_type=F32)


def forward_all(values, picked, out):
    tiles, slots = values.shape[:2]
    for t in range(tiles):
        one = forward_tile if t % 4 == 0 else forward_tile_vector
        out[t : t + 1, :] = one(values[t], picked[t * slots : (t + 1) * slots, :])


def back_all(values, rows_term, ids, out):
    tiles, slots = values.shape[:2]
    for t in range(tiles):
        block = slice(t * slots, (t + 1) * slots)
        out[block, :] = jnp.where(
            ids[block, :] >= 0.0, back_tile(values[t], rows_term[t : t + 1, :]), 0.0
        )


def first_kernel(share, columns_in, live_in, weights, values_in, values, ids, picked, own, along,
                 columns, live, weights_here, small_sem, values_sem):
    tiles, slots, rows, width = values.shape
    smalls = [
        pltpu.make_async_copy(columns_in, columns, small_sem.at[0]),
        pltpu.make_async_copy(live_in, live, small_sem.at[1]),
        pltpu.make_async_copy(weights, weights_here, small_sem.at[2]),
    ]
    for small in smalls:
        small.start()
    load = pltpu.make_async_copy(values_in, values, values_sem)
    load.start()
    for small in smalls:
        small.wait()
    for t in range(tiles):
        count = live[0, t]
        for j in range(slots):
            slot = t * slots + j
            column = columns[j, t]
            used = j < count
            row = weights_here[pl.ds(column, 1), :]
            picked[slot : slot + 1, :] = jnp.where(used, row, 0.0)
            ids[slot : slot + 1, :] = jnp.full(
                (1, width), jnp.where(used, column, -2), jnp.int32
            ).astype(F32)
    offset = pl.multiple_of(lax.axis_index("inst") * share, SUB)
    own[...] = weights_here[pl.ds(offset, share), :]
    load.wait()
    forward_all(values, picked, along)


def gradient_kernel(count, labels, values, ids, *refs):
    parts, (payload, curvature) = refs[:count], refs[count:]
    slots = ids.shape[0]
    margin = parts[0][...]
    for part in parts[1:]:
        margin = margin + part[...]
    prob = 1.0 / (1.0 + jnp.exp(-margin))
    curvature[...] = prob * (1.0 - prob)
    back_all(values, prob - labels[...].astype(F32), ids, payload)
    square = ids[...]
    diagonal = row_iota(square.shape) == lane_iota(square.shape)
    sent = jnp.sum(jnp.where(diagonal, square, 0.0), axis=0, keepdims=True)
    sent = jnp.where(sent < 0.0, -1.0, sent)
    payload[slots:, :] = jnp.broadcast_to(sent, (SUB, sent.shape[1]))


def stack_halves(parts, slots, halves):
    width = parts[0].shape[1]
    for k, part in enumerate(parts):
        block = part[:slots, :]
        high = block.astype(BF16)
        halves[k * slots : (k + 1) * slots, :width] = high
        halves[k * slots : (k + 1) * slots, width:] = (block - high.astype(F32)).astype(BF16)


def pick_sums(onehot, halves):
    both = jnp.dot(onehot, halves[...], preferred_element_type=F32)
    width = both.shape[1] // 2
    return both[:, :width] + both[:, width:]


def fill_onehot(ids, share, parts, onehot):
    slots, width = ids.shape
    offset = lax.axis_index("inst") * share
    blocks = (row_iota((share, width)) + offset).astype(F32)
    for k, part in enumerate(parts):
        sent = part[slots : slots + 1, :]
        place = slice(k * slots, (k + 1) * slots)
        onehot[:slots, place] = jnp.where(ids[...] == sent, 1.0, 0.0).astype(BF16)
        onehot[slots:, place] = jnp.where(blocks == sent, 1.0, 0.0).astype(BF16)


def start_early_kernel(count, share, ids, *refs):
    parts, (onehot, sums, halves) = refs[:count], refs[count:]
    fill_onehot(ids, share, parts, onehot)
    stack_halves(parts, ids.shape[0], halves)
    sums[...] = pick_sums(onehot[...], halves)


def start_kernel(count, values, ids, picked, own, early, *refs):
    parts = refs[:count]
    gradient, start_slot, onehot, payload, halves = refs[count:]
    tiles = values.shape[0]
    slots, width = ids.shape
    fill_onehot(ids, own.shape[0], parts, onehot)
    stack_halves(parts, slots, halves)
    start_slot[...] = -(picked[...] + early[:slots, :] + pick_sums(onehot[:slots, :], halves))
    slope = own[...] + early[slots:, :] + pick_sums(onehot[slots:, :], halves)
    gradient[...] = slope
    forward_all(values, start_slot, payload)
    payload[tiles:, :] = scalar_rows(width, total(slope * slope))


def curve_kernel(count, values, ids, curvature, *refs):
    parts, (along, payload) = refs[:count], refs[count:]
    tiles = values.shape[0]
    slots, width = ids.shape
    summed = parts[0][...]
    for part in parts[1:]:
        summed = summed + part[...]
    here = summed[:tiles, :]
    along[...] = here
    curved = curvature[...] * here
    back_all(values, curved, ids, payload)
    rounded = curved.astype(BF16).astype(F32)
    norm_part = summed[tiles : tiles + 1, 0:1]
    payload[slots:, :] = scalar_rows(width, norm_part, total(rounded * here))


def turn_early_kernel(count, onehot, *refs):
    parts, (sums, scalars, halves) = refs[:count], refs[count:]
    slots = parts[0].shape[0] - SUB
    stack_halves(parts, slots, halves)
    sums[...] = pick_sums(onehot[...], halves)
    scalars[...] = sum((part[slots:, :] for part in parts[1:]), parts[0][slots:, :])


def turn_kernel(count, values, onehot, start_slot, gradient, early, early_scalars, *refs):
    parts = refs[:count]
    next_share, known, payload, halves, next_slot = refs[count:]
    tiles = values.shape[0]
    slots, width = start_slot.shape
    scalars = early_scalars[...]
    for part in parts:
        scalars = scalars + part[slots:, :]
    norm_now = read_scalar(scalars[0:1, :], 0)
    curve_now = read_scalar(scalars[0:1, :], 1)
    alpha = norm_now / (norm_now + curve_now)
    stack_halves(parts, slots, halves)
    start = start_slot[...]
    summed = early[:slots, :] + pick_sums(onehot[:slots, :], halves)
    next_slot[...] = start - alpha * (start + summed)
    start_own = -gradient[...]
    summed = early[slots:, :] + pick_sums(onehot[slots:, :], halves)
    turned = start_own - alpha * (start_own + summed)
    next_share[...] = turned
    forward_all(values, next_slot, payload)
    payload[tiles:, :] = scalar_rows(width, total(turned * turned), total(turned * start_own))
    known[...] = scalar_rows(width, norm_now, curve_now, alpha)


def inner_kernel(count, curvature, along, *refs):
    parts, (scalars,) = refs[:count], refs[count:]
    tiles, width = along.shape
    summed = parts[0][...]
    for part in parts[1:]:
        summed = summed + part[...]
    turn = summed[:tiles, :]
    bent = curvature[...] * turn
    scalars[...] = scalar_rows(
        width,
        summed[tiles : tiles + 1, 0:1],
        summed[tiles : tiles + 1, 1:2],
        total(bent * turn),
        total(bent * along[...]),
    )


def last_kernel(known, gradient, next_share, *refs):
    parts, step = refs[:-1], refs[-1]
    row = parts[0][0:1, :]
    for part in parts[1:]:
        row = row + part[0:1, :]
    norm_next, cross, turn_turn, turn_along = (read_scalar(row, i) for i in range(4))
    row = known[0:1, :]
    norm_now, curve_now, alpha = (read_scalar(row, i) for i in range(3))
    ratio = norm_next / norm_now
    bottom = (
        norm_next
        + turn_turn
        + 2.0 * ratio * (cross + turn_along)
        + ratio * ratio * (norm_now + curve_now)
    )
    alpha_next = norm_next / bottom
    start = -gradient[...]
    step[...] = alpha * start + alpha_next * (next_share[...] + ratio * start)


def near(shape, dtype=F32):
    return pltpu.VMEM(shape, dtype)


def call(kernel, out_shape, args, in_specs=None, scratch_shapes=()):
    vmem = pl.BlockSpec(memory_space=pltpu.VMEM)
    if in_specs is None:
        in_specs = [vmem] * len(args)
        args = [pltpu.with_memory_space_constraint(a, pltpu.VMEM) for a in args]
    return pl.pallas_call(
        kernel,
        out_shape=out_shape,
        in_specs=in_specs,
        out_specs=jax.tree.map(lambda _: vmem, out_shape),
        scratch_shapes=list(scratch_shapes),
        compiler_params=pltpu.CompilerParams(vmem_limit_bytes=LIMIT),
    )(*args)


def swap(array, axis, distance):
    size = lax.axis_size(axis)
    return lax.ppermute(array, axis, [(i, i ^ distance) for i in range(size)])


def swap_both(array, distance):
    size, feats = lax.axis_size("inst"), lax.axis_size("feat")
    pairs = [
        (i * feats + f, (i ^ distance) * feats + (f ^ 1))
        for i in range(size)
        for f in range(feats)
    ]
    return lax.ppermute(array, ("inst", "feat"), pairs)


def feat_parts(array):
    distance = 1
    parts = [array]
    while distance < lax.axis_size("feat"):
        array = sum(parts[1:], parts[0])
        parts = [array, swap(array, "feat", distance | 1)]
        distance *= 2
    return parts


def inst_parts(array):
    size = lax.axis_size("inst")
    if size != 8:
        gathered = lax.all_gather(array, "inst", axis=0)
        return [gathered[i] for i in range(size)]
    parts = {0: array}
    for distance in (2, 4, 6, 1, 3):
        parts[distance] = swap(array, "inst", distance)
    for distance in (4, 6):
        parts[distance ^ 1] = swap(parts[distance], "inst", 1)
    return list(parts.values())


def inst_sum_parts(array):
    size = lax.axis_size("inst")
    stages = [(2, 4, 6), (1,)] if size == 8 else [(1 << b,) for b in range(size.bit_length() - 1)]
    parts = [array]
    for stage in stages:
        array = sum(parts[1:], parts[0])
        parts = [array] + [swap_both(array, distance) for distance in stage]
    return parts


def per_device(values, columns, live_slots, labels, weights):
    tiles, slots_of, rows, width = values.shape
    slots = tiles * slots_of
    share = weights.shape[0] // lax.axis_size("inst")
    insts, pair = lax.axis_size("inst"), 2

    values_here, ids, picked, own, part = call(
        functools.partial(first_kernel, share),
        (
            near(values.shape, BF16),
            near((slots, width)),
            near((slots, width)),
            near((share, width)),
            near((tiles, rows)),
        ),
        [
            pltpu.with_memory_space_constraint(a, pltpu.HBM)
            for a in (columns.T, live_slots.T, weights, values)
        ],
        in_specs=[pl.BlockSpec(memory_space=pltpu.HBM)] * 4,
        scratch_shapes=[
            pltpu.SMEM((slots_of, tiles), jnp.int32),
            pltpu.SMEM((1, tiles), jnp.int32),
            pltpu.VMEM(weights.shape, F32),
            pltpu.SemaphoreType.DMA((3,)),
            pltpu.SemaphoreType.DMA,
        ],
    )
    payload, curvature = call(
        functools.partial(gradient_kernel, pair),
        (near((slots + SUB, width)), near((tiles, rows))),
        (labels.reshape(tiles, rows), values_here, ids, *feat_parts(part)),
    )
    late = 2
    early = insts - late
    wanted = slots + share

    def halves(count):
        return pltpu.VMEM((count * slots, 2 * width), BF16)

    parts = inst_parts(payload)
    onehot_early, sums = call(
        functools.partial(start_early_kernel, early, share),
        (near((wanted, early * slots), BF16), near((wanted, width))),
        (ids, *parts[:early]),
        scratch_shapes=[halves(early)],
    )
    gradient, start_slot, onehot, payload = call(
        functools.partial(start_kernel, late),
        (
            near((share, width)),
            near((slots, width)),
            near((wanted, late * slots), BF16),
            near((tiles + SUB, rows)),
        ),
        (values_here, ids, picked, own, sums, *parts[early:]),
        scratch_shapes=[halves(late)],
    )
    along, payload = call(
        functools.partial(curve_kernel, pair),
        (near((tiles, rows)), near((slots + SUB, width))),
        (values_here, ids, curvature, *feat_parts(payload)),
    )
    parts = inst_parts(payload)
    sums, scalars = call(
        functools.partial(turn_early_kernel, early),
        (near((wanted, width)), near((SUB, width))),
        (onehot_early, *parts[:early]),
        scratch_shapes=[halves(early)],
    )
    next_share, known, payload = call(
        functools.partial(turn_kernel, late),
        (near((share, width)), near((SUB, width)), near((tiles + SUB, rows))),
        (values_here, onehot, start_slot, gradient, sums, scalars, *parts[early:]),
        scratch_shapes=[halves(late), pltpu.VMEM((slots, width), F32)],
    )
    scalars = call(
        functools.partial(inner_kernel, pair),
        near((SUB, width)),
        (curvature, along, *feat_parts(payload)),
    )
    step = call(
        last_kernel,
        near((share, width)),
        (known, gradient, next_share, *inst_sum_parts(scalars)),
    )
    return (step, gradient)


def solution(mesh):
    in_specs = (
        P("inst", "feat", None, None),
        P("inst", "feat"),
        P("inst", "feat"),
        P("inst"),
        P("feat", None),
    )
    out_specs = (P(("feat", "inst"), None), P(("feat", "inst"), None))
    return jax.shard_map(
        per_device, mesh=mesh, in_specs=in_specs, out_specs=out_specs, check_vma=False
    )
```

```python
import functools

import jax
import jax.numpy as jnp
from jax import lax
from jax.experimental import pallas as pl
from jax.experimental.pallas import tpu as pltpu
from jax.sharding import PartitionSpec as P

F32 = jnp.float32
BF16 = jnp.bfloat16
SUB = 8
LIMIT = 24 * 1024 * 1024


def row_iota(shape):
    return lax.broadcasted_iota(jnp.int32, shape, 0)


def lane_iota(shape):
    return lax.broadcasted_iota(jnp.int32, shape, 1)


def total(array):
    return jnp.sum(jnp.sum(array, axis=0, keepdims=True), axis=1, keepdims=True)


def scalar_rows(width, *scalars):
    lane = lane_iota((SUB, width))
    block = jnp.zeros((SUB, width), F32)
    for place, scalar in enumerate(scalars):
        block = jnp.where(lane == place, scalar, block)
    return block


def read_scalar(block, place):
    lane = lane_iota(block.shape)
    return jnp.sum(jnp.where(lane == place, block, 0.0), axis=1, keepdims=True)


def forward_tile_vector(tile, picked):
    picked = picked.astype(BF16).astype(F32)
    kept = tile[0].astype(F32) * picked[0:1, :]
    for s in range(1, tile.shape[0]):
        kept = kept + tile[s].astype(F32) * picked[s : s + 1, :]
    return jnp.sum(kept.T, axis=0, keepdims=True)


def forward_tile(tile, picked):
    slots, rows, width = tile.shape
    product = lax.dot_general(
        picked.astype(BF16),
        tile.reshape(slots * rows, width),
        (((1,), (1,)), ((), ())),
        preferred_element_type=F32,
    )
    mine = row_iota((slots, rows))
    kept = jnp.where(mine == 0, product[:, :rows], 0.0)
    for s in range(1, slots):
        kept = kept + jnp.where(mine == s, product[:, s * rows : (s + 1) * rows], 0.0)
    return jnp.sum(kept, axis=0, keepdims=True)


def back_tile(tile, rows_term):
    slots, rows, width = tile.shape
    mine = row_iota((slots, rows))
    spread = jnp.concatenate(
        [jnp.where(mine == s, rows_term, 0.0) for s in range(slots)], axis=1
    ).astype(BF16)
    return jnp.dot(spread, tile.reshape(slots * rows, width), preferred_element_type=F32)


def forward_all(values, picked, out):
    tiles, slots = values.shape[:2]
    for t in range(tiles):
        one = forward_tile if t % 4 == 0 else forward_tile_vector
        out[t : t + 1, :] = one(values[t], picked[t * slots : (t + 1) * slots, :])


def back_all(values, rows_term, ids, out):
    tiles, slots = values.shape[:2]
    for t in range(tiles):
        block = slice(t * slots, (t + 1) * slots)
        out[block, :] = jnp.where(
            ids[block, :] >= 0.0, back_tile(values[t], rows_term[t : t + 1, :]), 0.0
        )


def first_kernel(share, columns_in, live_in, weights, values_in, values, ids, picked, own, along,
                 columns, live, weights_here, small_sem, values_sem):
    tiles, slots, rows, width = values.shape
    smalls = [
        pltpu.make_async_copy(columns_in, columns, small_sem.at[0]),
        pltpu.make_async_copy(live_in, live, small_sem.at[1]),
        pltpu.make_async_copy(weights, weights_here, small_sem.at[2]),
    ]
    for small in smalls:
        small.start()
    load = pltpu.make_async_copy(values_in, values, values_sem)
    load.start()
    for small in smalls:
        small.wait()
    for t in range(tiles):
        count = live[0, t]
        for j in range(slots):
            slot = t * slots + j
            column = columns[j, t]
            used = j < count
            row = weights_here[pl.ds(column, 1), :]
            picked[slot : slot + 1, :] = jnp.where(used, row, 0.0)
            ids[slot : slot + 1, :] = jnp.full(
                (1, width), jnp.where(used, column, -2), jnp.int32
            ).astype(F32)
    offset = pl.multiple_of(lax.axis_index("inst") * share, SUB)
    own[...] = weights_here[pl.ds(offset, share), :]
    load.wait()
    forward_all(values, picked, along)


def gradient_kernel(count, labels, values, ids, *refs):
    parts, (payload, curvature) = refs[:count], refs[count:]
    slots = ids.shape[0]
    margin = parts[0][...]
    for part in parts[1:]:
        margin = margin + part[...]
    prob = 1.0 / (1.0 + jnp.exp(-margin))
    curvature[...] = prob * (1.0 - prob)
    back_all(values, prob - labels[...].astype(F32), ids, payload)
    square = ids[...]
    diagonal = row_iota(square.shape) == lane_iota(square.shape)
    sent = jnp.sum(jnp.where(diagonal, square, 0.0), axis=0, keepdims=True)
    sent = jnp.where(sent < 0.0, -1.0, sent)
    payload[slots:, :] = jnp.broadcast_to(sent, (SUB, sent.shape[1]))


def stack_halves(parts, slots, halves):
    width = parts[0].shape[1]
    for k, part in enumerate(parts):
        block = part[:slots, :]
        high = block.astype(BF16)
        halves[k * slots : (k + 1) * slots, :width] = high
        halves[k * slots : (k + 1) * slots, width:] = (block - high.astype(F32)).astype(BF16)


def pick_sums(onehot, halves):
    both = jnp.dot(onehot, halves[...], preferred_element_type=F32)
    width = both.shape[1] // 2
    return both[:, :width] + both[:, width:]


def fill_onehot(ids, share, parts, onehot):
    slots, width = ids.shape
    offset = lax.axis_index("inst") * share
    blocks = (row_iota((share, width)) + offset).astype(F32)
    for k, part in enumerate(parts):
        sent = part[slots : slots + 1, :]
        place = slice(k * slots, (k + 1) * slots)
        onehot[:slots, place] = jnp.where(ids[...] == sent, 1.0, 0.0).astype(BF16)
        onehot[slots:, place] = jnp.where(blocks == sent, 1.0, 0.0).astype(BF16)


def start_early_kernel(count, share, ids, *refs):
    parts, (onehot, sums, halves) = refs[:count], refs[count:]
    fill_onehot(ids, share, parts, onehot)
    stack_halves(parts, ids.shape[0], halves)
    sums[...] = pick_sums(onehot[...], halves)


def start_kernel(count, values, ids, picked, own, early, *refs):
    parts = refs[:count]
    gradient, start_slot, onehot, payload, halves = refs[count:]
    tiles = values.shape[0]
    slots, width = ids.shape
    fill_onehot(ids, own.shape[0], parts, onehot)
    stack_halves(parts, slots, halves)
    start_slot[...] = -(picked[...] + early[:slots, :] + pick_sums(onehot[:slots, :], halves))
    slope = own[...] + early[slots:, :] + pick_sums(onehot[slots:, :], halves)
    gradient[...] = slope
    forward_all(values, start_slot, payload)
    payload[tiles:, :] = scalar_rows(width, total(slope * slope))


def curve_kernel(count, values, ids, curvature, *refs):
    parts, (along, payload) = refs[:count], refs[count:]
    tiles = values.shape[0]
    slots, width = ids.shape
    summed = parts[0][...]
    for part in parts[1:]:
        summed = summed + part[...]
    here = summed[:tiles, :]
    along[...] = here
    curved = curvature[...] * here
    back_all(values, curved, ids, payload)
    rounded = curved.astype(BF16).astype(F32)
    norm_part = summed[tiles : tiles + 1, 0:1]
    payload[slots:, :] = scalar_rows(width, norm_part, total(rounded * here))


def turn_early_kernel(count, onehot, *refs):
    parts, (sums, scalars, halves) = refs[:count], refs[count:]
    slots = parts[0].shape[0] - SUB
    stack_halves(parts, slots, halves)
    sums[...] = pick_sums(onehot[...], halves)
    scalars[...] = sum((part[slots:, :] for part in parts[1:]), parts[0][slots:, :])


def turn_kernel(count, values, onehot, start_slot, gradient, early, early_scalars, *refs):
    parts = refs[:count]
    next_share, known, payload, halves, next_slot = refs[count:]
    tiles = values.shape[0]
    slots, width = start_slot.shape
    scalars = early_scalars[...]
    for part in parts:
        scalars = scalars + part[slots:, :]
    norm_now = read_scalar(scalars[0:1, :], 0)
    curve_now = read_scalar(scalars[0:1, :], 1)
    alpha = norm_now / (norm_now + curve_now)
    stack_halves(parts, slots, halves)
    start = start_slot[...]
    summed = early[:slots, :] + pick_sums(onehot[:slots, :], halves)
    next_slot[...] = start - alpha * (start + summed)
    start_own = -gradient[...]
    summed = early[slots:, :] + pick_sums(onehot[slots:, :], halves)
    turned = start_own - alpha * (start_own + summed)
    next_share[...] = turned
    forward_all(values, next_slot, payload)
    payload[tiles:, :] = scalar_rows(width, total(turned * turned), total(turned * start_own))
    known[...] = scalar_rows(width, norm_now, curve_now, alpha)


def inner_kernel(count, curvature, along, *refs):
    parts, (scalars,) = refs[:count], refs[count:]
    tiles, width = along.shape
    summed = parts[0][...]
    for part in parts[1:]:
        summed = summed + part[...]
    turn = summed[:tiles, :]
    bent = curvature[...] * turn
    scalars[...] = scalar_rows(
        width,
        summed[tiles : tiles + 1, 0:1],
        summed[tiles : tiles + 1, 1:2],
        total(bent * turn),
        total(bent * along[...]),
    )


def last_kernel(known, gradient, next_share, *refs):
    parts, step = refs[:-1], refs[-1]
    row = parts[0][0:1, :]
    for part in parts[1:]:
        row = row + part[0:1, :]
    norm_next, cross, turn_turn, turn_along = (read_scalar(row, i) for i in range(4))
    row = known[0:1, :]
    norm_now, curve_now, alpha = (read_scalar(row, i) for i in range(3))
    ratio = norm_next / norm_now
    bottom = (
        norm_next
        + turn_turn
        + 2.0 * ratio * (cross + turn_along)
        + ratio * ratio * (norm_now + curve_now)
    )
    alpha_next = norm_next / bottom
    start = -gradient[...]
    step[...] = alpha * start + alpha_next * (next_share[...] + ratio * start)


def near(shape, dtype=F32):
    return pltpu.VMEM(shape, dtype)


def call(kernel, out_shape, args, in_specs=None, scratch_shapes=()):
    vmem = pl.BlockSpec(memory_space=pltpu.VMEM)
    if in_specs is None:
        in_specs = [vmem] * len(args)
        args = [pltpu.with_memory_space_constraint(a, pltpu.VMEM) for a in args]
    return pl.pallas_call(
        kernel,
        out_shape=out_shape,
        in_specs=in_specs,
        out_specs=jax.tree.map(lambda _: vmem, out_shape),
        scratch_shapes=list(scratch_shapes),
        compiler_params=pltpu.CompilerParams(vmem_limit_bytes=LIMIT),
    )(*args)


def swap(array, axis, distance):
    size = lax.axis_size(axis)
    return lax.ppermute(array, axis, [(i, i ^ distance) for i in range(size)])


def swap_both(array, distance):
    size, feats = lax.axis_size("inst"), lax.axis_size("feat")
    pairs = [
        (i * feats + f, (i ^ distance) * feats + (f ^ 1))
        for i in range(size)
        for f in range(feats)
    ]
    return lax.ppermute(array, ("inst", "feat"), pairs)


def feat_parts(array):
    distance = 1
    parts = [array]
    while distance < lax.axis_size("feat"):
        array = sum(parts[1:], parts[0])
        parts = [array, swap(array, "feat", distance | 1)]
        distance *= 2
    return parts


def inst_parts(array):
    size = lax.axis_size("inst")
    if size != 8:
        gathered = lax.all_gather(array, "inst", axis=0)
        return [gathered[i] for i in range(size)]
    parts = {0: array}
    for distance in (6, 4, 3, 1, 2):
        parts[distance] = swap(array, "inst", distance)
    for distance in (6, 4):
        parts[distance ^ 1] = swap(parts[distance], "inst", 1)
    return list(parts.values())


def inst_sum_parts(array):
    size = lax.axis_size("inst")
    stages = [(2, 4, 6), (1,)] if size == 8 else [(1 << b,) for b in range(size.bit_length() - 1)]
    parts = [array]
    for stage in stages:
        array = sum(parts[1:], parts[0])
        parts = [array] + [swap_both(array, distance) for distance in stage]
    return parts


def per_device(values, columns, live_slots, labels, weights):
    tiles, slots_of, rows, width = values.shape
    slots = tiles * slots_of
    share = weights.shape[0] // lax.axis_size("inst")
    insts, pair = lax.axis_size("inst"), 2

    values_here, ids, picked, own, part = call(
        functools.partial(first_kernel, share),
        (
            near(values.shape, BF16),
            near((slots, width)),
            near((slots, width)),
            near((share, width)),
            near((tiles, rows)),
        ),
        [
            pltpu.with_memory_space_constraint(a, pltpu.HBM)
            for a in (columns.T, live_slots.T, weights, values)
        ],
        in_specs=[pl.BlockSpec(memory_space=pltpu.HBM)] * 4,
        scratch_shapes=[
            pltpu.SMEM((slots_of, tiles), jnp.int32),
            pltpu.SMEM((1, tiles), jnp.int32),
            pltpu.VMEM(weights.shape, F32),
            pltpu.SemaphoreType.DMA((3,)),
            pltpu.SemaphoreType.DMA,
        ],
    )
    payload, curvature = call(
        functools.partial(gradient_kernel, pair),
        (near((slots + SUB, width)), near((tiles, rows))),
        (labels.reshape(tiles, rows), values_here, ids, *feat_parts(part)),
    )
    late = 2
    early = insts - late
    wanted = slots + share

    def halves(count):
        return pltpu.VMEM((count * slots, 2 * width), BF16)

    parts = inst_parts(payload)
    onehot_early, sums = call(
        functools.partial(start_early_kernel, early, share),
        (near((wanted, early * slots), BF16), near((wanted, width))),
        (ids, *parts[:early]),
        scratch_shapes=[halves(early)],
    )
    gradient, start_slot, onehot, payload = call(
        functools.partial(start_kernel, late),
        (
            near((share, width)),
            near((slots, width)),
            near((wanted, late * slots), BF16),
            near((tiles + SUB, rows)),
        ),
        (values_here, ids, picked, own, sums, *parts[early:]),
        scratch_shapes=[halves(late)],
    )
    along, payload = call(
        functools.partial(curve_kernel, pair),
        (near((tiles, rows)), near((slots + SUB, width))),
        (values_here, ids, curvature, *feat_parts(payload)),
    )
    parts = inst_parts(payload)
    sums, scalars = call(
        functools.partial(turn_early_kernel, early),
        (near((wanted, width)), near((SUB, width))),
        (onehot_early, *parts[:early]),
        scratch_shapes=[halves(early)],
    )
    next_share, known, payload = call(
        functools.partial(turn_kernel, late),
        (near((share, width)), near((SUB, width)), near((tiles + SUB, rows))),
        (values_here, onehot, start_slot, gradient, sums, scalars, *parts[early:]),
        scratch_shapes=[halves(late), pltpu.VMEM((slots, width), F32)],
    )
    scalars = call(
        functools.partial(inner_kernel, pair),
        near((SUB, width)),
        (curvature, along, *feat_parts(payload)),
    )
    step = call(
        last_kernel,
        near((share, width)),
        (known, gradient, next_share, *inst_sum_parts(scalars)),
    )
    return (step, gradient)


def solution(mesh):
    in_specs = (
        P("inst", "feat", None, None),
        P("inst", "feat"),
        P("inst", "feat"),
        P("inst"),
        P("feat", None),
    )
    out_specs = (P(("feat", "inst"), None), P(("feat", "inst"), None))
    return jax.shard_map(
        per_device, mesh=mesh, in_specs=in_specs, out_specs=out_specs, check_vma=False
    )
```

```python
import functools

import jax
import jax.numpy as jnp
from jax import lax
from jax.experimental import pallas as pl
from jax.experimental.pallas import tpu as pltpu
from jax.sharding import PartitionSpec as P

F32 = jnp.float32
BF16 = jnp.bfloat16
SUB = 8
LIMIT = 24 * 1024 * 1024


def row_iota(shape):
    return lax.broadcasted_iota(jnp.int32, shape, 0)


def lane_iota(shape):
    return lax.broadcasted_iota(jnp.int32, shape, 1)


def total(array):
    return jnp.sum(jnp.sum(array, axis=0, keepdims=True), axis=1, keepdims=True)


def scalar_rows(width, *scalars):
    lane = lane_iota((SUB, width))
    block = jnp.zeros((SUB, width), F32)
    for place, scalar in enumerate(scalars):
        block = jnp.where(lane == place, scalar, block)
    return block


def read_scalar(block, place):
    lane = lane_iota(block.shape)
    return jnp.sum(jnp.where(lane == place, block, 0.0), axis=1, keepdims=True)


def forward_tile_vector(tile, picked):
    picked = picked.astype(BF16).astype(F32)
    kept = tile[0].astype(F32) * picked[0:1, :]
    for s in range(1, tile.shape[0]):
        kept = kept + tile[s].astype(F32) * picked[s : s + 1, :]
    return jnp.sum(kept.T, axis=0, keepdims=True)


def forward_tile(tile, picked):
    slots, rows, width = tile.shape
    product = lax.dot_general(
        picked.astype(BF16),
        tile.reshape(slots * rows, width),
        (((1,), (1,)), ((), ())),
        preferred_element_type=F32,
    )
    mine = row_iota((slots, rows))
    kept = jnp.where(mine == 0, product[:, :rows], 0.0)
    for s in range(1, slots):
        kept = kept + jnp.where(mine == s, product[:, s * rows : (s + 1) * rows], 0.0)
    return jnp.sum(kept, axis=0, keepdims=True)


def back_tile(tile, rows_term):
    slots, rows, width = tile.shape
    mine = row_iota((slots, rows))
    spread = jnp.concatenate(
        [jnp.where(mine == s, rows_term, 0.0) for s in range(slots)], axis=1
    ).astype(BF16)
    return jnp.dot(spread, tile.reshape(slots * rows, width), preferred_element_type=F32)


def forward_all(values, picked, out):
    tiles, slots = values.shape[:2]
    for t in range(tiles):
        one = forward_tile if t % 4 == 0 else forward_tile_vector
        out[t : t + 1, :] = one(values[t], picked[t * slots : (t + 1) * slots, :])


def back_all(values, rows_term, ids, out):
    tiles, slots = values.shape[:2]
    for t in range(tiles):
        block = slice(t * slots, (t + 1) * slots)
        out[block, :] = jnp.where(
            ids[block, :] >= 0.0, back_tile(values[t], rows_term[t : t + 1, :]), 0.0
        )


def first_kernel(share, columns_in, live_in, weights, values_in, values, ids, picked, own, along,
                 columns, live, weights_here, small_sem, values_sem):
    tiles, slots, rows, width = values.shape
    smalls = [
        pltpu.make_async_copy(columns_in, columns, small_sem.at[0]),
        pltpu.make_async_copy(live_in, live, small_sem.at[1]),
        pltpu.make_async_copy(weights, weights_here, small_sem.at[2]),
    ]
    for small in smalls:
        small.start()
    load = pltpu.make_async_copy(values_in, values, values_sem)
    load.start()
    for small in smalls:
        small.wait()
    def gather(t, carry):
        count = live[0, t]
        base = pl.multiple_of(t * slots, SUB)
        for j in range(slots):
            column = columns[j, t]
            used = j < count
            row = weights_here[pl.ds(column, 1), :]
            picked[pl.ds(base + j, 1), :] = jnp.where(used, row, 0.0)
            ids[pl.ds(base + j, 1), :] = jnp.full(
                (1, width), jnp.where(used, column, -2), jnp.int32
            ).astype(F32)
        return carry

    lax.fori_loop(0, tiles, gather, 0)
    offset = pl.multiple_of(lax.axis_index("inst") * share, SUB)
    own[...] = weights_here[pl.ds(offset, share), :]
    load.wait()
    forward_all(values, picked, along)


def gradient_kernel(count, labels, values, ids, *refs):
    parts, (payload, curvature) = refs[:count], refs[count:]
    slots = ids.shape[0]
    margin = parts[0][...]
    for part in parts[1:]:
        margin = margin + part[...]
    prob = 1.0 / (1.0 + jnp.exp(-margin))
    curvature[...] = prob * (1.0 - prob)
    back_all(values, prob - labels[...].astype(F32), ids, payload)
    square = ids[...]
    diagonal = row_iota(square.shape) == lane_iota(square.shape)
    sent = jnp.sum(jnp.where(diagonal, square, 0.0), axis=0, keepdims=True)
    sent = jnp.where(sent < 0.0, -1.0, sent)
    payload[slots:, :] = jnp.broadcast_to(sent, (SUB, sent.shape[1]))


def stack_halves(parts, slots, halves):
    width = parts[0].shape[1]
    for k, part in enumerate(parts):
        block = part[:slots, :]
        high = block.astype(BF16)
        halves[k * slots : (k + 1) * slots, :width] = high
        halves[k * slots : (k + 1) * slots, width:] = (block - high.astype(F32)).astype(BF16)


def pick_sums(onehot, halves):
    both = jnp.dot(onehot, halves[...], preferred_element_type=F32)
    width = both.shape[1] // 2
    return both[:, :width] + both[:, width:]


def fill_onehot(ids, share, parts, onehot):
    slots, width = ids.shape
    offset = lax.axis_index("inst") * share
    blocks = (row_iota((share, width)) + offset).astype(F32)
    for k, part in enumerate(parts):
        sent = part[slots : slots + 1, :]
        place = slice(k * slots, (k + 1) * slots)
        onehot[:slots, place] = jnp.where(ids[...] == sent, 1.0, 0.0).astype(BF16)
        onehot[slots:, place] = jnp.where(blocks == sent, 1.0, 0.0).astype(BF16)


def start_early_kernel(count, share, ids, *refs):
    parts, (onehot, sums, halves) = refs[:count], refs[count:]
    fill_onehot(ids, share, parts, onehot)
    stack_halves(parts, ids.shape[0], halves)
    sums[...] = pick_sums(onehot[...], halves)


def start_kernel(count, values, ids, picked, own, early, *refs):
    parts = refs[:count]
    gradient, start_slot, onehot, payload, halves = refs[count:]
    tiles = values.shape[0]
    slots, width = ids.shape
    fill_onehot(ids, own.shape[0], parts, onehot)
    stack_halves(parts, slots, halves)
    start_slot[...] = -(picked[...] + early[:slots, :] + pick_sums(onehot[:slots, :], halves))
    slope = own[...] + early[slots:, :] + pick_sums(onehot[slots:, :], halves)
    gradient[...] = slope
    forward_all(values, start_slot, payload)
    payload[tiles:, :] = scalar_rows(width, total(slope * slope))


def curve_kernel(count, values, ids, curvature, *refs):
    parts, (along, payload) = refs[:count], refs[count:]
    tiles = values.shape[0]
    slots, width = ids.shape
    summed = parts[0][...]
    for part in parts[1:]:
        summed = summed + part[...]
    here = summed[:tiles, :]
    along[...] = here
    curved = curvature[...] * here
    back_all(values, curved, ids, payload)
    rounded = curved.astype(BF16).astype(F32)
    norm_part = summed[tiles : tiles + 1, 0:1]
    payload[slots:, :] = scalar_rows(width, norm_part, total(rounded * here))


def turn_early_kernel(count, onehot, *refs):
    parts, (sums, scalars, halves) = refs[:count], refs[count:]
    slots = parts[0].shape[0] - SUB
    stack_halves(parts, slots, halves)
    sums[...] = pick_sums(onehot[...], halves)
    scalars[...] = sum((part[slots:, :] for part in parts[1:]), parts[0][slots:, :])


def turn_kernel(count, values, onehot, start_slot, gradient, early, early_scalars, *refs):
    parts = refs[:count]
    next_share, known, payload, halves, next_slot = refs[count:]
    tiles = values.shape[0]
    slots, width = start_slot.shape
    scalars = early_scalars[...]
    for part in parts:
        scalars = scalars + part[slots:, :]
    norm_now = read_scalar(scalars[0:1, :], 0)
    curve_now = read_scalar(scalars[0:1, :], 1)
    alpha = norm_now / (norm_now + curve_now)
    stack_halves(parts, slots, halves)
    start = start_slot[...]
    summed = early[:slots, :] + pick_sums(onehot[:slots, :], halves)
    next_slot[...] = start - alpha * (start + summed)
    start_own = -gradient[...]
    summed = early[slots:, :] + pick_sums(onehot[slots:, :], halves)
    turned = start_own - alpha * (start_own + summed)
    next_share[...] = turned
    forward_all(values, next_slot, payload)
    payload[tiles:, :] = scalar_rows(width, total(turned * turned), total(turned * start_own))
    known[...] = scalar_rows(width, norm_now, curve_now, alpha)


def inner_kernel(count, curvature, along, *refs):
    parts, (scalars,) = refs[:count], refs[count:]
    tiles, width = along.shape
    summed = parts[0][...]
    for part in parts[1:]:
        summed = summed + part[...]
    turn = summed[:tiles, :]
    bent = curvature[...] * turn
    scalars[...] = scalar_rows(
        width,
        summed[tiles : tiles + 1, 0:1],
        summed[tiles : tiles + 1, 1:2],
        total(bent * turn),
        total(bent * along[...]),
    )


def last_kernel(known, gradient, next_share, *refs):
    parts, step = refs[:-1], refs[-1]
    row = parts[0][0:1, :]
    for part in parts[1:]:
        row = row + part[0:1, :]
    norm_next, cross, turn_turn, turn_along = (read_scalar(row, i) for i in range(4))
    row = known[0:1, :]
    norm_now, curve_now, alpha = (read_scalar(row, i) for i in range(3))
    ratio = norm_next / norm_now
    bottom = (
        norm_next
        + turn_turn
        + 2.0 * ratio * (cross + turn_along)
        + ratio * ratio * (norm_now + curve_now)
    )
    alpha_next = norm_next / bottom
    start = -gradient[...]
    step[...] = alpha * start + alpha_next * (next_share[...] + ratio * start)


def near(shape, dtype=F32):
    return pltpu.VMEM(shape, dtype)


def call(kernel, out_shape, args, in_specs=None, scratch_shapes=()):
    vmem = pl.BlockSpec(memory_space=pltpu.VMEM)
    if in_specs is None:
        in_specs = [vmem] * len(args)
        args = [pltpu.with_memory_space_constraint(a, pltpu.VMEM) for a in args]
    return pl.pallas_call(
        kernel,
        out_shape=out_shape,
        in_specs=in_specs,
        out_specs=jax.tree.map(lambda _: vmem, out_shape),
        scratch_shapes=list(scratch_shapes),
        compiler_params=pltpu.CompilerParams(vmem_limit_bytes=LIMIT),
    )(*args)


def swap(array, axis, distance):
    size = lax.axis_size(axis)
    return lax.ppermute(array, axis, [(i, i ^ distance) for i in range(size)])


def swap_both(array, distance):
    size, feats = lax.axis_size("inst"), lax.axis_size("feat")
    pairs = [
        (i * feats + f, (i ^ distance) * feats + (f ^ 1))
        for i in range(size)
        for f in range(feats)
    ]
    return lax.ppermute(array, ("inst", "feat"), pairs)


def feat_parts(array):
    distance = 1
    parts = [array]
    while distance < lax.axis_size("feat"):
        array = sum(parts[1:], parts[0])
        parts = [array, swap(array, "feat", distance | 1)]
        distance *= 2
    return parts


def inst_parts(array):
    size = lax.axis_size("inst")
    if size != 8:
        gathered = lax.all_gather(array, "inst", axis=0)
        return [gathered[i] for i in range(size)]
    parts = {0: array}
    for distance in (6, 4, 3, 1, 2):
        parts[distance] = swap(array, "inst", distance)
    for distance in (6, 4):
        parts[distance ^ 1] = swap(parts[distance], "inst", 1)
    return list(parts.values())


def inst_sum_parts(array):
    size = lax.axis_size("inst")
    stages = [(2, 4, 6), (1,)] if size == 8 else [(1 << b,) for b in range(size.bit_length() - 1)]
    parts = [array]
    for stage in stages:
        array = sum(parts[1:], parts[0])
        parts = [array] + [swap_both(array, distance) for distance in stage]
    return parts


def per_device(values, columns, live_slots, labels, weights):
    tiles, slots_of, rows, width = values.shape
    slots = tiles * slots_of
    share = weights.shape[0] // lax.axis_size("inst")
    insts, pair = lax.axis_size("inst"), 2

    values_here, ids, picked, own, part = call(
        functools.partial(first_kernel, share),
        (
            near(values.shape, BF16),
            near((slots, width)),
            near((slots, width)),
            near((share, width)),
            near((tiles, rows)),
        ),
        [
            pltpu.with_memory_space_constraint(a, pltpu.HBM)
            for a in (columns.T, live_slots.T, weights, values)
        ],
        in_specs=[pl.BlockSpec(memory_space=pltpu.HBM)] * 4,
        scratch_shapes=[
            pltpu.SMEM((slots_of, tiles), jnp.int32),
            pltpu.SMEM((1, tiles), jnp.int32),
            pltpu.VMEM(weights.shape, F32),
            pltpu.SemaphoreType.DMA((3,)),
            pltpu.SemaphoreType.DMA,
        ],
    )
    payload, curvature = call(
        functools.partial(gradient_kernel, pair),
        (near((slots + SUB, width)), near((tiles, rows))),
        (labels.reshape(tiles, rows), values_here, ids, *feat_parts(part)),
    )
    late = 2
    early = insts - late
    wanted = slots + share

    def halves(count):
        return pltpu.VMEM((count * slots, 2 * width), BF16)

    parts = inst_parts(payload)
    onehot_early, sums = call(
        functools.partial(start_early_kernel, early, share),
        (near((wanted, early * slots), BF16), near((wanted, width))),
        (ids, *parts[:early]),
        scratch_shapes=[halves(early)],
    )
    gradient, start_slot, onehot, payload = call(
        functools.partial(start_kernel, late),
        (
            near((share, width)),
            near((slots, width)),
            near((wanted, late * slots), BF16),
            near((tiles + SUB, rows)),
        ),
        (values_here, ids, picked, own, sums, *parts[early:]),
        scratch_shapes=[halves(late)],
    )
    along, payload = call(
        functools.partial(curve_kernel, pair),
        (near((tiles, rows)), near((slots + SUB, width))),
        (values_here, ids, curvature, *feat_parts(payload)),
    )
    parts = inst_parts(payload)
    sums, scalars = call(
        functools.partial(turn_early_kernel, early),
        (near((wanted, width)), near((SUB, width))),
        (onehot_early, *parts[:early]),
        scratch_shapes=[halves(early)],
    )
    next_share, known, payload = call(
        functools.partial(turn_kernel, late),
        (near((share, width)), near((SUB, width)), near((tiles + SUB, rows))),
        (values_here, onehot, start_slot, gradient, sums, scalars, *parts[early:]),
        scratch_shapes=[halves(late), pltpu.VMEM((slots, width), F32)],
    )
    scalars = call(
        functools.partial(inner_kernel, pair),
        near((SUB, width)),
        (curvature, along, *feat_parts(payload)),
    )
    step = call(
        last_kernel,
        jax.ShapeDtypeStruct((share, width), F32),
        (known, gradient, next_share, *inst_sum_parts(scalars)),
    )
    return (step, gradient)


def solution(mesh):
    in_specs = (
        P("inst", "feat", None, None),
        P("inst", "feat"),
        P("inst", "feat"),
        P("inst"),
        P("feat", None),
    )
    out_specs = (P(("feat", "inst"), None), P(("feat", "inst"), None))
    return jax.shard_map(
        per_device, mesh=mesh, in_specs=in_specs, out_specs=out_specs, check_vma=False
    )
```
